32 devices in a mesh: rows: 8 (over z, x), feat: 4 (over y, core).
Axes of the slice: x: 2, y: 2, z: 4, core: 2. Of those that a mesh axis runs over, the one named last changes fastest.
Arguments:
- band_feats: float32 [4096, 1024], P('rows', 'feat'), may hold values from -6 to 6
- head_feats: float32 [512, 1024], P('rows', 'feat'), may hold values from -6 to 6
- mix_weights: bfloat16 [2, 1024, 1024], P(None, None, 'feat'), may hold values from -0.1875 to 0.1875
- tile_place: int32 [256, 3], P('rows'), may hold values from -1 to 3, as said below
- tile_vals: bfloat16 [256, 128, 128], P('rows'), may hold values from -1 to 1
- arrow_cols: bfloat16 [4096, 512], P('rows'), may hold values from -1 to 1
- arrow_reach: int32 [4096], P('rows'), may hold values from 1 to 512
- arrow_rows: bfloat16 [512, 4096], P(None, 'rows'), may hold values from -0.5 to 0.5
- band_degree: int32 [4096], P('rows'), may hold values from 8 to 32
- head_degree: int32 [512], replicated, may hold values from 8 to 32
Outputs:
- band_out: float32 [4096, 1024], P('rows', 'feat')
- head_out: float32 [512, 1024], P('rows', 'feat')
The draws below stay inside these ranges and needn't reach their ends.
Inputs may be any that keep to these rules, and one draw needn't show every extreme that they name: `tile_place`: row and column lie in 0 to 3 and the offset in -1 to 1; the 32 slots of every block hold offsets -1, 0 and 1.
All inputs are finite; a program needn't handle non-finite values.
Results may differ from the reference program's by a relative error of at most 0.0057.
Values may be sent and summed in bfloat16 or wider, within the bound.
No kernel may reach another device: no remote copies, remote signals or barrier semaphores. Data moves between devices by JAX's collectives and lax.ppermute only.
A program may use at most 64 MiB of HBM per device.

```python
import jax
import jax.numpy as jnp
from jax import lax

F = 1024
ARROW = 512
TILE = 128
TPR = 8
ITERS = 2
ROWS_DEV = 512
TPD = 32
NB = 4096


def draw_tile_place(key, part):
    blocks = NB // ROWS_DEV
    tile_rows = ROWS_DEV // TILE
    key_row, key_col, key_off = jax.random.split(key, 3)
    row_pick = jax.random.randint(key_row, (blocks, TPD), 0, tile_rows)
    col_pick = jax.random.randint(key_col, (blocks, TPD), 0, tile_rows)
    off_pick = jax.random.randint(key_off, (blocks, TPD), -1, 2)
    slot = jnp.broadcast_to(jnp.arange(TPD, dtype=jnp.int32)[None, :], (blocks, TPD))
    off_pick = jnp.where(slot == 0, -1, jnp.where(slot == 1, 1, jnp.where(slot == 2, 0, off_pick)))
    row_pick = jnp.where(slot == 2, tile_rows - 1, row_pick)
    col_pick = jnp.where(slot == 2, tile_rows - 1, col_pick)
    stacked = jnp.stack([row_pick, col_pick, off_pick], axis=-1)
    return stacked.reshape(blocks * TPD, 3).astype(jnp.int32)


def with_ends(entries, rng, low, top_value):
    longest = entries.shape.index(max(entries.shape))
    spots = []
    for shift in (0, 1):
        where = [jax.random.randint(jax.random.fold_in(rng, axis), (), 0, length) for axis, length in enumerate(entries.shape)]
        where[longest] = (where[longest] + shift) % entries.shape[longest]
        spots.append(tuple(where))
    return entries.at[spots[0]].set(low).at[spots[1]].set(top_value)


def block_scale(stream_key, dims, shards, least, top_value):
    def one(position, parts):
        heights = jax.random.uniform(jax.random.fold_in(jax.random.fold_in(stream_key, 6), position), (parts,), jnp.float32, least / len(shards), top_value / len(shards))
        return jnp.repeat(jnp.exp(heights), dims[position] // parts).reshape((-1,) + (1,) * (len(dims) - position - 1))

    level = one(*shards[0])
    for cut in shards[1:]:
        level = level * one(*cut)
    return level


def bell_draw(stream_key, shape, spread, reach, pieces=(), kind=jnp.bfloat16):
    drawn = jax.random.normal(stream_key, shape, jnp.float32) * spread
    if len(pieces) > 0:
        drawn = block_scale(stream_key, shape, pieces, -0.22, 0.18) * drawn
    return jnp.clip(drawn, min=-reach, max=reach).astype(kind)


def setup_inputs(seed: int = 0) -> dict:
    key_list = jax.random.split(jax.random.key(seed), 11)
    band_feats = bell_draw(key_list[0], (NB, F), 1.0, 6.0, ((0, 8), (1, 4)), jnp.float32)
    head_feats = bell_draw(key_list[1], (ARROW, F), 1.0, 6.0, ((0, 8), (1, 4)), jnp.float32)
    mix_weights = bell_draw(key_list[2], (ITERS, F, F), F ** -0.5, 0.1875, ((2, 4),))
    tile_place = draw_tile_place(jax.random.fold_in(key_list[10], 71), 0)
    tile_vals = bell_draw(key_list[4], (NB // TILE * TPR, TILE, TILE), ((TPR * TILE + ARROW // 2) // 35) ** -0.5, 1.0, ((0, 8),))
    arrow_cols = bell_draw(key_list[5], (NB, ARROW), ((TPR * TILE + ARROW // 2) // 35) ** -0.5, 1.0, ((0, 8),))
    arrow_reach = with_ends(jax.random.randint(key_list[6], (NB,), 1, ARROW + 1), jax.random.fold_in(key_list[6], 1), 1, ARROW).astype(jnp.int32)
    arrow_rows = bell_draw(key_list[7], (ARROW, NB), (NB // 35) ** -0.5, 0.5, ((1, 8),))
    band_degree = with_ends(jax.random.randint(key_list[8], (NB,), 8, 33), jax.random.fold_in(key_list[8], 1), 8, 32).astype(jnp.int32)
    head_degree = with_ends(jax.random.randint(key_list[9], (ARROW,), 8, 33), jax.random.fold_in(key_list[9], 1), 8, 32).astype(jnp.int32)
    return {"band_feats": band_feats, "head_feats": head_feats, "mix_weights": mix_weights, "tile_place": tile_place, "tile_vals": tile_vals, "arrow_cols": arrow_cols, "arrow_reach": arrow_reach, "arrow_rows": arrow_rows, "band_degree": band_degree, "head_degree": head_degree}


def band_product(band_x, tile_place, tile_vals):
    blocks = NB // ROWS_DEV
    tile_rows = ROWS_DEV // TILE
    padded = jnp.concatenate([jnp.zeros((ROWS_DEV, F), jnp.bfloat16), band_x, jnp.zeros((ROWS_DEV, F), jnp.bfloat16)], axis=0)

    def one_block(inputs):
        block_pos, places, values = inputs
        window = lax.dynamic_slice_in_dim(padded, (block_pos * ROWS_DEV).astype(jnp.int32), 3 * ROWS_DEV, 0)
        window = window.reshape(3 * tile_rows, TILE, F)
        column = (places[:, 2] + 1) * tile_rows + places[:, 1]
        picked = window[column].astype(jnp.float32)
        products = jnp.einsum('sij,sjf->sif', values.astype(jnp.float32), picked, precision=lax.Precision.HIGHEST)
        onehot = (places[:, 0][None, :] == jnp.arange(tile_rows, dtype=jnp.int32)[:, None]).astype(jnp.float32)
        summed = jnp.einsum('rs,sif->rif', onehot, products, precision=lax.Precision.HIGHEST)
        return summed.reshape(ROWS_DEV, F)
    result = lax.map(one_block, (jnp.arange(blocks, dtype=jnp.int32), tile_place.reshape(blocks, TPD, 3), tile_vals.reshape(blocks, TPD, TILE, TILE)))
    return result.reshape(NB, F)

def reference(band_feats, head_feats, mix_weights, tile_place, tile_vals, arrow_cols, arrow_reach, arrow_rows, band_degree, head_degree):
    reach_mask = jnp.arange(ARROW, dtype=jnp.int32)[None, :] < arrow_reach[:, None]
    masked_cols = jnp.where(reach_mask, arrow_cols, jnp.zeros_like(arrow_cols))
    band_scale = lax.rsqrt(band_degree.astype(jnp.float32))[:, None]
    head_scale = lax.rsqrt(head_degree.astype(jnp.float32))[:, None]
    band_state, head_state = (band_feats, head_feats)
    for layer_step in range(ITERS):
        mixing = mix_weights[layer_step]
        band_x = jnp.dot(band_state.astype(jnp.bfloat16), mixing, preferred_element_type=jnp.float32).astype(jnp.bfloat16)
        head_x = jnp.dot(head_state.astype(jnp.bfloat16), mixing, preferred_element_type=jnp.float32).astype(jnp.bfloat16)
        band_sum = band_product(band_x, tile_place, tile_vals) + jnp.dot(masked_cols, head_x, preferred_element_type=jnp.float32)
        head_sum = jnp.dot(arrow_rows, band_x, preferred_element_type=jnp.float32)
        band_state = jnp.maximum(band_sum * band_scale, 0.0)
        head_state = jnp.maximum(head_sum * head_scale, 0.0)
    return (band_state, head_state)
```

```python
import functools

import jax
import jax.numpy as jnp
from jax import lax
from jax.experimental import pallas as pl
from jax.experimental.pallas import tpu as pltpu
from jax.sharding import PartitionSpec as P

BF = jnp.bfloat16
F32 = jnp.float32
LIMIT = 28 * 1024 * 1024


def local(kernel, outs, scalars, args, scratch=(), flops=0):
    vmem = pl.BlockSpec(memory_space=pltpu.VMEM)
    smem = pl.BlockSpec(memory_space=pltpu.SMEM)
    moved = sum(a.size * a.dtype.itemsize for a in args)
    return pl.pallas_call(
        kernel,
        out_shape=[jax.ShapeDtypeStruct(s, d) for s, d in outs],
        in_specs=[smem] * len(scalars) + [vmem] * len(args),
        out_specs=[vmem] * len(outs),
        scratch_shapes=list(scratch),
        cost_estimate=pl.CostEstimate(flops=flops, bytes_accessed=moved, transcendentals=0),
        compiler_params=pltpu.CompilerParams(vmem_limit_bytes=LIMIT),
    )(*scalars, *args)


def mm(a, b):
    return jnp.dot(a, b, preferred_element_type=F32)


def swap(cells, axis, bit):
    count = lax.axis_size(axis)
    return lax.ppermute(cells, axis, [(i, i ^ bit) for i in range(count)])


def forward(cells):
    count = lax.axis_size("rows")
    pairs = []
    for i in range(count):
        if i % 2 == 0:
            pairs.append((i, i + 2 if i + 2 < count else i + 1))
        else:
            pairs.append((i, i - 2 if i > 1 else 0))
    return lax.ppermute(cells, "rows", pairs)


def spread(axis, cells, bits):
    pieces = {0: cells}
    for bit in bits:
        pieces.update({k | bit: swap(c, axis, bit) for k, c in list(pieces.items())})
    return pieces


def column(values, width):
    wide = jnp.broadcast_to(values.astype(F32), (128, values.shape[1]))
    tall = wide.T
    return jnp.concatenate([tall] * (width // 128), axis=1) if width > 128 else tall


def after(value, *others):
    return lax.optimization_barrier((value, *others))[0]


def split_partial(where, part, keep, send, head_dev):
    if not head_dev:
        keep[...] = part[...]
        return
    pair, parity = where[0] // 2, where[0] % 2
    for k in range(keep.shape[0] // head_dev):
        mine = pl.multiple_of((2 * (pair ^ k) + parity) * head_dev, head_dev)
        theirs = pl.multiple_of((2 * (pair ^ k) + 1 - parity) * head_dev, head_dev)
        keep[k * head_dev : (k + 1) * head_dev] = part[pl.ds(mine, head_dev)]
        send[k * head_dev : (k + 1) * head_dev] = part[pl.ds(theirs, head_dev)].astype(BF)


def begin_kernel(where, band, head, rows, out, head_out, keep, part, *, head_dev):
    size = band.shape[0]
    out[:size] = band[...].astype(BF)
    head_out[...] = head[...].astype(BF)
    part[...] = mm(rows[...], out[:size])
    split_partial(where, part, keep, out.at[size:] if head_dev else None, head_dev)


def dense_kernel(where, place, tiles, cols, reach, cells, near, pair, far, masked, own, window, *, blocks):
    tile = tiles.shape[1]
    rows = window.shape[0]
    tile_rows = rows // tile
    parity = where[0] % 2
    toward = 1 - 2 * parity
    inside = jnp.logical_and(where[0] != 0, where[0] != blocks - 1)
    window[...] = jnp.zeros_like(window)

    def add(s, carry):
        offset = place[s, 2]
        group = jnp.where(offset == 0, 0, jnp.where(offset == toward, 1, 2))

        @pl.when(jnp.logical_or(group != 2, inside))
        def _():
            r = pl.ds(pl.multiple_of(place[s, 0] * tile, tile), tile)
            c = pl.ds(pl.multiple_of((group * tile_rows + place[s, 1]) * tile, tile), tile)
            window[r, c] += tiles[s].astype(F32)

        return carry

    lax.fori_loop(0, tiles.shape[0], add, 0)
    near[...] = window[:, :rows].astype(BF)
    pair[...] = window[:, rows : 2 * rows].astype(BF)
    far[...] = window[:, 2 * rows :].astype(BF)
    limit = column(reach[...], 128)
    for g in range(cols.shape[1] // 128):
        here = slice(g * 128, (g + 1) * 128)
        lane = (lax.broadcasted_iota(jnp.int32, (rows, 128), 1) + g * 128).astype(F32)
        masked[:, here] = jnp.where(lane < limit, cols[:, here].astype(F32), 0.0).astype(BF)
    own[...] = mm(near[...], cells[:rows])


def near_kernel(near, cells, out):
    out[...] = mm(near[...], cells[: out.shape[0]])


def add_kernel(total, weight, cells, out):
    out[...] = total[...] + mm(weight[...], cells[: out.shape[0]])


def heads_kernel(where, total, masked, mine, theirs, out, heads, *, head_dev):
    whole_heads(where, mine, theirs, heads, head_dev)
    out[...] = total[...] + mm(masked[...], heads[...])


def fold_kernel(keep, arrived, onward, *outs):
    size = outs[0].shape[0]
    skip = onward.shape[0]
    onward[...] = arrived[:skip]
    for k, out in enumerate(outs):
        here = keep[k * size : (k + 1) * size]
        out[...] = (here + arrived[skip + k * size : skip + (k + 1) * size].astype(F32)).astype(out.dtype)


def join_kernel(*refs):
    size = refs[0].shape[0]
    for k, ref in enumerate(refs[:-1]):
        refs[-1][k * size : (k + 1) * size] = ref[...]


def whole_heads(where, mine, theirs, heads, head_dev):
    if not head_dev:
        heads[...] = mine[...]
        return
    pair, parity = where[0] // 2, where[0] % 2
    for k in range(mine.shape[0] // head_dev):
        here = slice(k * head_dev, (k + 1) * head_dev)
        a = pl.multiple_of((2 * (pair ^ k) + parity) * head_dev, head_dev)
        b = pl.multiple_of((2 * (pair ^ k) + 1 - parity) * head_dev, head_dev)
        heads[pl.ds(a, head_dev)] = mine[here]
        heads[pl.ds(b, head_dev)] = theirs[here]


def first_sum_kernel(total, far, other, *refs):
    parts, out = refs[:-1], refs[-1]
    rows = total.shape[0]
    out[:rows] = (total[...] + mm(far[...], other[...])).astype(BF)
    if parts:
        extra = parts[0][...]
        for part in parts[1:]:
            extra = extra + part[...].astype(F32)
        out[rows:] = extra.astype(BF)


def last_sum_kernel(total, far, other, scale, out):
    out[...] = jnp.maximum((total[...] + mm(far[...], other[...])) * scale[...], 0.0)


def mix_begin_kernel(where, *refs, order, early):
    pieces, shards, outs = refs[:early], refs[early : early + len(order)], refs[early + len(order) :]
    width = pieces[0].shape[1]
    for shard, out in zip(shards, outs):
        total = None
        for k, piece in zip(order, pieces):
            rows = pl.ds(pl.multiple_of((where[1] ^ k) * width, width), width)
            term = mm(piece[...], shard[rows])
            total = term if total is None else total + term
        out[...] = total


def mix_end_kernel(where, *refs, order, early, head_dev):
    count = len(order)
    late = count - early
    pieces, shards, begun = refs[:late], refs[late : late + count], refs[late + count : late + 2 * count]
    refs = refs[late + 2 * count :]
    if head_dev:
        weights, rows, degree, head_degree, out, keep, band_scale, head_out, part, scale, head_scale = refs
    else:
        weights, rows, degree, out, keep, band_scale, part, scale = refs
    band, width = band_scale.shape
    band_scale[...] = lax.rsqrt(column(degree[...], width))
    scale[:band] = band_scale[...]
    if head_dev:
        head_scale[...] = lax.rsqrt(column(head_degree[...], width))
        scale[band:] = head_scale[pl.ds(pl.multiple_of(where[0] * head_dev, head_dev), head_dev)]
    result = None
    for j, shard, total in zip(order, shards, begun):
        total = total[...]
        for k, piece in zip(order[early:], pieces):
            here = pl.ds(pl.multiple_of((where[1] ^ k) * width, width), width)
            total = total + mm(piece[...], shard[here])
        state = jnp.maximum(total * scale[...], 0.0).astype(BF)
        here = pl.ds(pl.multiple_of((where[1] ^ j) * width, width), width)
        term = mm(state, weights[1, here])
        result = term if result is None else result + term
    out[:band] = result[:band].astype(BF)
    if head_dev:
        head_out[...] = result[band:].astype(BF)
    part[...] = mm(rows[...], out[:band])
    split_partial(where, part, keep, out.at[band:] if head_dev else None, head_dev)


def head_out_kernel(where, own, *refs):
    arrived, (degree, out, scales) = refs[:-3], refs[-3:]
    total = own[...]
    for ref in arrived:
        total = total + ref[...].astype(F32)
    size = out.shape[0]
    scales[...] = lax.rsqrt(column(degree[...], out.shape[1]))
    out[...] = jnp.maximum(total * scales[pl.ds(pl.multiple_of(where[0] * size, size), size)], 0.0)


def body(
    band_feats,
    head_feats,
    mix_weights,
    tile_place,
    tile_vals,
    arrow_cols,
    arrow_reach,
    arrow_rows,
    band_degree,
    head_degree,
):
    rows_dev, width = band_feats.shape
    head_dev = head_feats.shape[0]
    heads = arrow_cols.shape[1]
    blocks = lax.axis_size("rows")
    pairs = blocks // 2
    top_bit = lax.axis_size("feat") // 2
    low_bits = [1 << n for n in reversed(range(top_bit.bit_length() - 1))]
    where = jnp.stack([lax.axis_index("rows"), lax.axis_index("feat")]).astype(jnp.int32)
    reach = arrow_reach[None, :]
    band_deg = band_degree[None, :]
    head_deg = head_degree[None, :]
    size = head_dev if pairs <= 4 and head_dev % 16 == 0 else 0
    part_rows = heads // 2 if size else heads
    part_scratch = pltpu.VMEM((heads, width), F32)
    head_scratch = pltpu.VMEM((heads, width), BF)
    band_sum = [((rows_dev, width), F32)]
    keep_shape = ((part_rows, width), F32)
    sent = ((rows_dev + (part_rows if size else 0), width), BF)
    heads_add = functools.partial(heads_kernel, head_dev=size)

    def z_pieces(parts):
        return [swap(parts[k], "rows", 2 * k) for k in range(1, pairs)]

    def gather_heads(own, before):
        if not size:
            everyone = lax.all_gather(own, "rows", axis=0, tiled=True)
            return everyone, everyone
        others = z_pieces([own] * pairs)
        (mine,) = local(join_kernel, [((part_rows, width), BF)], (), (after(own, before), *others))
        return mine, swap(mine, "rows", 1)

    def hand_on(keep, arrived, before):
        if not size:
            return forward(arrived), []
        keep = after(keep, before)
        outs = [((rows_dev, width), BF), ((size, width), F32)] + [((size, width), BF)] * (pairs - 1)
        onward, *parts = local(fold_kernel, outs, (), (keep, arrived))
        return forward(onward), [parts[0]] + z_pieces(parts)

    cells, head_cells, keep = local(
        functools.partial(begin_kernel, head_dev=size),
        [sent, ((head_dev, width), BF), keep_shape],
        (where,),
        (band_feats, head_feats, arrow_rows),
        [part_scratch],
    )
    first_part = keep
    pair_cells = swap(cells, "rows", 1)
    first = after(mix_weights, keep)[0]
    near, pair, far, masked, total = local(
        functools.partial(dense_kernel, blocks=blocks),
        [((rows_dev, rows_dev), BF)] * 3 + [((rows_dev, heads), BF), ((rows_dev, width), F32)],
        (where, tile_place),
        (tile_vals, arrow_cols, reach, cells),
        [pltpu.VMEM((rows_dev, 3 * rows_dev), F32)],
    )
    shards = spread("feat", first, [top_bit] + low_bits)
    mine, theirs = gather_heads(head_cells, total)
    far_cells, parts = hand_on(keep, pair_cells, mine)
    (total,) = local(add_kernel, band_sum, (), (after(total, *parts[:1]), pair, pair_cells))
    (total,) = local(heads_add, band_sum, (where,), (total, masked, mine, theirs), [head_scratch])
    (joined,) = local(
        first_sum_kernel, [((rows_dev + size, width), BF)], (), (total, far, far_cells, *parts)
    )

    near_pieces = spread("feat", joined, low_bits)
    opposite = swap(joined, "feat", top_bit)
    order = tuple(sorted(shards))
    weights = [shards[k] for k in order]
    early = len(near_pieces)
    begun = local(
        functools.partial(mix_begin_kernel, order=order, early=early),
        [((rows_dev + size, width), F32)] * len(order),
        (where,),
        (*[near_pieces[k] for k in order[:early]], *weights),
    )
    far_pieces = spread("feat", after(opposite, *begun), low_bits)
    degrees = (band_deg, head_deg) if size else (band_deg,)
    scratch = [part_scratch, pltpu.VMEM((rows_dev + size, width), F32)]
    cells, keep, scale, *head_x = local(
        functools.partial(mix_end_kernel, order=order, early=early, head_dev=size),
        [sent, keep_shape] + band_sum + ([((size, width), BF)] if size else []),
        (where,),
        (*[far_pieces[k ^ top_bit] for k in order[early:]], *weights, *begun, mix_weights, arrow_rows, *degrees),
        scratch + ([pltpu.VMEM((heads, width), F32)] if size else []),
    )
    if not size:
        own_scale = lax.dynamic_slice_in_dim(
            lax.rsqrt(head_degree.astype(F32)), lax.axis_index("rows") * head_dev, head_dev, 0
        )[:, None]
        summed = lax.psum_scatter(first_part, "rows", scatter_dimension=0, tiled=True).astype(BF)
        summed = lax.all_gather(summed, "feat", axis=1, tiled=True)
        full = lax.all_gather(mix_weights[0], "feat", axis=1, tiled=True)
        head_x = [mm(jnp.maximum(mm(summed, full) * own_scale, 0.0).astype(BF), mix_weights[1]).astype(BF)]

    pair_cells = swap(cells, "rows", 1)
    (total,) = local(near_kernel, band_sum, (), (near, cells))
    mine, theirs = gather_heads(head_x[0], total)
    far_cells, parts = hand_on(keep, pair_cells, mine)
    (total,) = local(add_kernel, band_sum, (), (after(total, *parts[:1]), pair, pair_cells))
    (total,) = local(heads_add, band_sum, (where,), (total, masked, mine, theirs), [head_scratch])
    (band_out,) = local(last_sum_kernel, band_sum, (), (total, far, far_cells, scale))
    if size:
        (head_out,) = local(
            head_out_kernel,
            [((head_dev, width), F32)],
            (where,),
            (*parts, head_deg),
            [pltpu.VMEM((heads, width), F32)],
        )
    else:
        head_out = jnp.maximum(lax.psum_scatter(keep, "rows", scatter_dimension=0, tiled=True) * own_scale, 0.0)
    return band_out, head_out


def solution(mesh):
    in_specs = (
        P("rows", "feat"),
        P("rows", "feat"),
        P(None, None, "feat"),
        P("rows", None),
        P("rows", None, None),
        P("rows", None),
        P("rows"),
        P(None, "rows"),
        P("rows"),
        P(),
    )
    out_specs = (P("rows", "feat"), P("rows", "feat"))
    return jax.shard_map(body, mesh=mesh, in_specs=in_specs, out_specs=out_specs, check_vma=False)
```

```python
import functools

import jax
import jax.numpy as jnp
from jax import lax
from jax.experimental import pallas as pl
from jax.experimental.pallas import tpu as pltpu
from jax.sharding import PartitionSpec as P

BF = jnp.bfloat16
F32 = jnp.float32
LIMIT = 16 * 1024 * 1024
COST = 500_000_000


def local(kernel, outs, scalars, args, scratch=(), flops=COST):
    vmem = pl.BlockSpec(memory_space=pltpu.VMEM)
    smem = pl.BlockSpec(memory_space=pltpu.SMEM)
    moved = sum(a.size * a.dtype.itemsize for a in args)
    return pl.pallas_call(
        kernel,
        out_shape=[jax.ShapeDtypeStruct(s, d) for s, d in outs],
        in_specs=[smem] * len(scalars) + [vmem] * len(args),
        out_specs=[vmem] * len(outs),
        scratch_shapes=list(scratch),
        cost_estimate=pl.CostEstimate(flops=flops, bytes_accessed=moved, transcendentals=0),
        compiler_params=pltpu.CompilerParams(vmem_limit_bytes=LIMIT),
    )(*scalars, *args)


def mm(a, b):
    return jnp.dot(a, b, preferred_element_type=F32)


def swap(cells, axis, bit):
    count = lax.axis_size(axis)
    return lax.ppermute(cells, axis, [(i, i ^ bit) for i in range(count)])


def forward(cells):
    count = lax.axis_size("rows")
    pairs = []
    for i in range(count):
        if i % 2 == 0:
            pairs.append((i, i + 2 if i + 2 < count else i + 1))
        else:
            pairs.append((i, i - 2 if i > 1 else 0))
    return lax.ppermute(cells, "rows", pairs)


def spread(axis, cells, bits):
    pieces = {0: cells}
    for bit in bits:
        pieces.update({k | bit: swap(c, axis, bit) for k, c in list(pieces.items())})
    return pieces


def column(values, width):
    wide = jnp.broadcast_to(values.astype(F32), (128, values.shape[1]))
    tall = wide.T
    return jnp.concatenate([tall] * (width // 128), axis=1) if width > 128 else tall


def after(value, *others):
    return lax.optimization_barrier((value, *others))[0]


def xor_order(count):
    order = [0]
    bit = count // 2
    while bit:
        order += [k | bit for k in order]
        bit //= 2
    return order


def split_partial(part, keep, send, head_dev):
    if not head_dev:
        keep[...] = part[...]
        send[...] = part[...].astype(BF)
        return
    pair, parity = lax.axis_index("rows") // 2, lax.axis_index("rows") % 2
    for n, k in enumerate(xor_order(keep.shape[0] // head_dev)):
        mine = pl.multiple_of((2 * (pair ^ k) + parity) * head_dev, head_dev)
        theirs = pl.multiple_of((2 * (pair ^ k) + 1 - parity) * head_dev, head_dev)
        keep[n * head_dev : (n + 1) * head_dev] = part[pl.ds(mine, head_dev)]
        send[n * head_dev : (n + 1) * head_dev] = part[pl.ds(theirs, head_dev)].astype(BF)


def cast_kernel(cells, out):
    out[...] = cells[...].astype(BF)


def partial_kernel(rows, cells, *refs, head_dev):
    keep, send, part = refs[-3:]
    if len(refs) > 3:
        refs[1][...] = refs[0][...].astype(BF)
    part[...] = mm(rows[...], cells[...])
    split_partial(part, keep, send, head_dev)


def dense_kernel(place, tiles, cols, reach, cells, near, pair, far, masked, own, window, *, blocks):
    tile = tiles.shape[1]
    rows = window.shape[0]
    tile_rows = rows // tile
    parity = lax.axis_index("rows") % 2
    toward = 1 - 2 * parity
    inside = jnp.logical_and(lax.axis_index("rows") != 0, lax.axis_index("rows") != blocks - 1)
    window[...] = jnp.zeros_like(window)

    def add(s, carry):
        offset = place[2, s]
        group = jnp.where(offset == 0, 0, jnp.where(offset == toward, 1, 2))

        @pl.when(jnp.logical_or(group != 2, inside))
        def _():
            r = pl.ds(pl.multiple_of(place[0, s] * tile, tile), tile)
            c = pl.ds(pl.multiple_of((group * tile_rows + place[1, s]) * tile, tile), tile)
            window[r, c] += tiles[s].astype(F32)

        return carry

    lax.fori_loop(0, tiles.shape[0], add, 0)
    near[...] = window[:, :rows].astype(BF)
    pair[...] = window[:, rows : 2 * rows].astype(BF)
    far[...] = window[:, 2 * rows :].astype(BF)
    limit = column(reach[...], 128)
    for g in range(cols.shape[1] // 128):
        here = slice(g * 128, (g + 1) * 128)
        lane = (lax.broadcasted_iota(jnp.int32, (rows, 128), 1) + g * 128).astype(F32)
        masked[:, here] = jnp.where(lane < limit, cols[:, here].astype(F32), 0.0).astype(BF)
    own[...] = mm(near[...], cells[...])


def near_kernel(near, cells, out):
    out[...] = mm(near[...], cells[...])


def sum_kernel(total, pair, cells, masked, mine, theirs, out, heads, *, head_dev):
    whole_heads(mine, theirs, heads, head_dev)
    out[...] = total[...] + mm(pair[...], cells[...]) + mm(masked[...], heads[...])


def fold_kernel(keep, arrived, kept, send):
    half = kept.shape[0]
    kept[...] = keep[:half] + arrived[:half].astype(F32)
    send[...] = (keep[half:] + arrived[half:].astype(F32)).astype(BF)


def join_kernel(*refs):
    size = refs[0].shape[0]
    for k, ref in enumerate(refs[:-1]):
        refs[-1][k * size : (k + 1) * size] = ref[...]


def whole_heads(mine, theirs, heads, head_dev):
    if not head_dev:
        heads[...] = mine[...]
        return
    pair, parity = lax.axis_index("rows") // 2, lax.axis_index("rows") % 2
    for n, k in enumerate(xor_order(mine.shape[0] // head_dev)):
        here = slice(n * head_dev, (n + 1) * head_dev)
        a = pl.multiple_of((2 * (pair ^ k) + parity) * head_dev, head_dev)
        b = pl.multiple_of((2 * (pair ^ k) + 1 - parity) * head_dev, head_dev)
        heads[pl.ds(a, head_dev)] = mine[here]
        heads[pl.ds(b, head_dev)] = theirs[here]


def first_sum_kernel(total, far, other, *refs):
    parts, out = refs[:-1], refs[-1]
    rows = total.shape[0]
    out[:rows] = (total[...] + mm(far[...], other[...])).astype(BF)
    if parts:
        extra = parts[0][...]
        for part in parts[1:]:
            extra = extra + part[...].astype(F32)
        out[rows:] = extra.astype(BF)


def last_sum_kernel(total, far, other, scale, out):
    out[...] = jnp.maximum((total[...] + mm(far[...], other[...])) * scale[...], 0.0)


def feature_rows(k, width):
    return pl.ds(pl.multiple_of((lax.axis_index("feat") ^ k) * width, width), width)


def mix_begin_kernel(*refs, early):
    pieces, shards, outs = refs[:early], refs[early : early + 2], refs[early + 2 :]
    for shard, out in zip(shards, outs):
        total = None
        for k, piece in enumerate(pieces):
            term = mm(piece[...], shard[feature_rows(k, out.shape[1])])
            total = term if total is None else total + term
        out[...] = total


def mix_end_kernel(*refs, early, order, head_dev):
    pieces, refs = refs[: 2 * early], refs[2 * early :]
    shards, refs = refs[: 2 * early], refs[2 * early :]
    begun, refs = refs[:2], refs[2:]
    weights, band_scale, head_scale, *outs, scale = refs
    band, width = band_scale.shape
    scale[:band] = band_scale[...]
    if head_dev:
        scale[band:] = head_scale[...]
    result = None
    for n, (j, shard) in enumerate(zip(order, shards)):
        total = begun[n][...] if n < 2 else None
        for k in range(early if n < 2 else 0, 2 * early):
            term = mm(pieces[k][...], shard[feature_rows(k, width)])
            total = term if total is None else total + term
        state = jnp.maximum(total * scale[...], 0.0).astype(BF)
        term = mm(state, weights[1, feature_rows(j, width)])
        result = term if result is None else result + term
    outs[0][...] = result[:band].astype(BF)
    if head_dev:
        outs[1][...] = result[band:].astype(BF)


def scale_kernel(degree, head_degree, scale, head_scale, all_scales):
    size = head_scale.shape[0]
    scale[...] = lax.rsqrt(column(degree[...], scale.shape[1]))
    all_scales[...] = lax.rsqrt(column(head_degree[...], scale.shape[1]))
    head_scale[...] = all_scales[pl.ds(pl.multiple_of(lax.axis_index("rows") * size, size), size)]


def wide_scale_kernel(degree, scale):
    scale[...] = lax.rsqrt(column(degree[...], scale.shape[1]))


def head_out_kernel(own, *refs):
    arrived, (scale, out) = refs[:-2], refs[-2:]
    total = own[...]
    for ref in arrived:
        total = total + ref[...].astype(F32)
    out[...] = jnp.maximum(total * scale[...], 0.0)


def body(
    band_feats,
    head_feats,
    mix_weights,
    tile_place,
    tile_vals,
    arrow_cols,
    arrow_reach,
    arrow_rows,
    band_degree,
    head_degree,
):
    rows_dev, width = band_feats.shape
    head_dev = head_feats.shape[0]
    heads = arrow_cols.shape[1]
    blocks = lax.axis_size("rows")
    pairs = blocks // 2
    top_bit = lax.axis_size("feat") // 2
    low_bits = [1 << n for n in reversed(range(top_bit.bit_length() - 1))]
    reach = arrow_reach[None, :]
    size = head_dev if pairs <= 4 and head_dev % 16 == 0 else 0
    part_rows = heads // 2 if size else heads
    part_scratch = pltpu.VMEM((heads, width), F32)
    head_scratch = pltpu.VMEM((heads, width), BF)
    band_sum = [((rows_dev, width), F32)]
    cells_shape = ((rows_dev, width), BF)
    head_sum = ((head_dev, width), F32)
    keep_shapes = [((part_rows, width), F32), ((part_rows, width), BF)]
    sum_up = functools.partial(sum_kernel, head_dev=size)

    def partial_sums(cells, *head):
        outs = [(h.shape, BF) for h in head] + keep_shapes
        add_up = functools.partial(partial_kernel, head_dev=size)
        return local(add_up, outs, (), (arrow_rows, cells, *head), [part_scratch])

    def gather_heads(own, before):
        if not size:
            everyone = lax.all_gather(own, "rows", axis=0, tiled=True)
            return everyone, everyone
        mine = own
        bit = pairs // 2
        while bit:
            other = swap(mine, "rows", 2 * bit)
            rows = 2 * mine.shape[0]
            (mine,) = local(join_kernel, [((rows, width), BF)], (), (after(mine, before), other))
            bit //= 2
        return mine, swap(mine, "rows", 1)

    def scatter_heads(keep, send, before):
        if not size:
            return []
        bit = 1
        while bit <= pairs:
            arrived = swap(send, "rows", bit)
            if bit < pairs:
                rows = keep.shape[0] // 2
                outs = [((rows, width), F32), ((rows, width), BF)]
                keep, send = local(fold_kernel, outs, (), (after(keep, before), arrived))
            bit *= 2
        return [keep, arrived]

    (cells,) = local(cast_kernel, [cells_shape], (), (band_feats,))
    pair_cells = swap(cells, "rows", 1)
    first = after(mix_weights, cells)[0]
    across = swap(first, "feat", top_bit)
    head_cells, keep, send = partial_sums(cells, head_feats)
    first_part = keep
    near, pair, far, masked, total = local(
        functools.partial(dense_kernel, blocks=blocks),
        [((rows_dev, rows_dev), BF)] * 3 + [((rows_dev, heads), BF), ((rows_dev, width), F32)],
        (tile_place.T,),
        (tile_vals, arrow_cols, reach, after(cells, keep)),
        [pltpu.VMEM((rows_dev, 3 * rows_dev), F32)],
    )
    mine, theirs = gather_heads(head_cells, total)
    far_cells = forward(after(pair_cells, mine))
    parts = scatter_heads(keep, send, mine)
    total = after(total, *parts[:1])
    (total,) = local(sum_up, band_sum, (), (total, pair, pair_cells, masked, mine, theirs), [head_scratch])
    tall = rows_dev + size
    (joined,) = local(
        first_sum_kernel, [((tall, width), BF)], (), (total, far, far_cells, *parts)
    )

    opposite = swap(joined, "feat", top_bit)
    band_degree = after(band_degree, joined)
    if size:
        scale, head_scale = local(
            scale_kernel,
            band_sum + [head_sum],
            (),
            (band_degree[None, :], head_degree[None, :]),
            [pltpu.VMEM((heads, width), F32)],
        )
    else:
        (scale,) = local(wide_scale_kernel, band_sum, (), (band_degree[None, :],))
        head_scale = lax.rsqrt(head_degree.astype(F32))[:, None] * jnp.ones((1, width), F32)
        head_scale = lax.dynamic_slice_in_dim(head_scale, lax.axis_index("rows") * head_dev, head_dev, 0)
    pieces = spread("feat", after(joined, scale), low_bits)
    early = len(pieces)
    pieces.update({k | top_bit: c for k, c in spread("feat", opposite, low_bits).items()})
    pieces = [pieces[k] for k in sorted(pieces)]
    shards = spread("feat", after(first, scale), low_bits)
    shards.update({k | top_bit: w for k, w in spread("feat", after(across, scale), low_bits).items()})
    order = [0, top_bit] + [k for k in sorted(shards) if k not in (0, top_bit)]
    begun = local(
        functools.partial(mix_begin_kernel, early=early),
        [((tall, width), F32)] * 2,
        (),
        (after(pieces[0], opposite), *pieces[1:early], shards[0], shards[top_bit]),
    )
    cells, *head_x = local(
        functools.partial(mix_end_kernel, early=early, order=order, head_dev=size),
        [cells_shape] + ([((size, width), BF)] if size else []),
        (),
        (*pieces, *[shards[k] for k in order], *begun, mix_weights, scale, head_scale),
        [pltpu.VMEM((tall, width), F32)],
    )
    if not size:
        summed = lax.psum_scatter(first_part, "rows", scatter_dimension=0, tiled=True).astype(BF)
        summed = lax.all_gather(summed, "feat", axis=1, tiled=True)
        full = lax.all_gather(mix_weights[0], "feat", axis=1, tiled=True)
        head_state = jnp.maximum(mm(summed, full) * head_scale[:, :1], 0.0).astype(BF)
        head_x = [mm(head_state, mix_weights[1]).astype(BF)]

    pair_cells = swap(cells, "rows", 1)
    keep, send = partial_sums(cells)
    (total,) = local(near_kernel, band_sum, (), (after(near, keep), cells))
    mine, theirs = gather_heads(after(head_x[0], keep), total)
    far_cells = forward(after(pair_cells, mine))
    parts = scatter_heads(keep, send, mine)
    (total,) = local(
        sum_up, band_sum, (), (after(total, *parts[:1]), pair, pair_cells, masked, mine, theirs), [head_scratch]
    )
    if size:
        (head_out,) = local(head_out_kernel, [head_sum], (), (after(parts[0], total), *parts[1:], head_scale))
    else:
        head_out = jnp.maximum(lax.psum_scatter(keep, "rows", scatter_dimension=0, tiled=True) * head_scale, 0.0)
    (band_out,) = local(last_sum_kernel, band_sum, (), (total, far, far_cells, scale))
    return band_out, head_out


def solution(mesh):
    in_specs = (
        P("rows", "feat"),
        P("rows", "feat"),
        P(None, None, "feat"),
        P("rows", None),
        P("rows", None, None),
        P("rows", None),
        P("rows"),
        P(None, "rows"),
        P("rows"),
        P(),
    )
    out_specs = (P("rows", "feat"), P("rows", "feat"))
    return jax.shard_map(body, mesh=mesh, in_specs=in_specs, out_specs=out_specs, check_vma=False)
```

```python
import functools

import jax
import jax.numpy as jnp
from jax import lax
from jax.experimental import pallas as pl
from jax.experimental.pallas import tpu as pltpu
from jax.sharding import PartitionSpec as P

BF = jnp.bfloat16
F32 = jnp.float32
LIMIT = 16 * 1024 * 1024
WORK = {
    "cast": 500_000_000,
    "part1": 500_000_000,
    "dense": 500_000_000,
    "join1": 500_000_000,
    "fold1": 2_000_000_000,
    "sum1": 1_000_000,
    "first": 500_000_000,
    "scale": 500_000_000,
    "begin": 1_000_000_000,
    "mid": 500_000_000,
    "end": 500_000_000,
    "part2": 1_000_000,
    "near": 500_000_000,
    "join2": 500_000_000,
    "fold2": 500_000_000,
    "sum2": 500_000_000,
    "last": 500_000_000,
    "headout": 1_000_000,
}


def local(name, kernel, outs, scalars, args, scratch=()):
    vmem = pl.BlockSpec(memory_space=pltpu.VMEM)
    smem = pl.BlockSpec(memory_space=pltpu.SMEM)
    moved = sum(a.size * a.dtype.itemsize for a in args)
    return pl.pallas_call(
        kernel,
        out_shape=[jax.ShapeDtypeStruct(s, d) for s, d in outs],
        in_specs=[smem] * len(scalars) + [vmem] * len(args),
        out_specs=[vmem] * len(outs),
        scratch_shapes=list(scratch),
        cost_estimate=pl.CostEstimate(flops=WORK[name], bytes_accessed=moved, transcendentals=0),
        compiler_params=pltpu.CompilerParams(vmem_limit_bytes=LIMIT),
    )(*scalars, *args)


def mm(a, b):
    return jnp.dot(a, b, preferred_element_type=F32)


def swap(cells, axis, bit):
    count = lax.axis_size(axis)
    return lax.ppermute(cells, axis, [(i, i ^ bit) for i in range(count)])


def forward(cells):
    count = lax.axis_size("rows")
    pairs = []
    for i in range(count):
        if i % 2 == 0:
            pairs.append((i, i + 2 if i + 2 < count else i + 1))
        else:
            pairs.append((i, i - 2 if i > 1 else 0))
    return lax.ppermute(cells, "rows", pairs)


def spread(axis, cells, bits):
    pieces = {0: cells}
    for bit in bits:
        pieces.update({k | bit: swap(c, axis, bit) for k, c in list(pieces.items())})
    return pieces


def column(values, width):
    wide = jnp.broadcast_to(values.astype(F32), (128, values.shape[1]))
    tall = wide.T
    return jnp.concatenate([tall] * (width // 128), axis=1) if width > 128 else tall


def after(value, *others):
    return lax.optimization_barrier((value, *others))[0]


def xor_order(count):
    order = [0]
    bit = count // 2
    while bit:
        order += [k | bit for k in order]
        bit //= 2
    return order


def split_partial(part, keep, send, head_dev):
    if not head_dev:
        keep[...] = part[...]
        send[...] = part[...].astype(BF)
        return
    pair, parity = lax.axis_index("rows") // 2, lax.axis_index("rows") % 2
    for n, k in enumerate(xor_order(keep.shape[0] // head_dev)):
        mine = pl.multiple_of((2 * (pair ^ k) + parity) * head_dev, head_dev)
        theirs = pl.multiple_of((2 * (pair ^ k) + 1 - parity) * head_dev, head_dev)
        keep[n * head_dev : (n + 1) * head_dev] = part[pl.ds(mine, head_dev)]
        send[n * head_dev : (n + 1) * head_dev] = part[pl.ds(theirs, head_dev)].astype(BF)


def cast_kernel(cells, out):
    out[...] = cells[...].astype(BF)


def partial_kernel(rows, cells, *refs, head_dev):
    keep, send, part = refs[-3:]
    if len(refs) > 3:
        refs[1][...] = refs[0][...].astype(BF)
    part[...] = mm(rows[...], cells[...])
    split_partial(part, keep, send, head_dev)


def dense_kernel(place, tiles, cols, reach, cells, near, pair, far, masked, own, window, *, blocks):
    tile = tiles.shape[1]
    rows = window.shape[0]
    tile_rows = rows // tile
    parity = lax.axis_index("rows") % 2
    toward = 1 - 2 * parity
    inside = jnp.logical_and(lax.axis_index("rows") != 0, lax.axis_index("rows") != blocks - 1)
    window[...] = jnp.zeros_like(window)

    def add(s, carry):
        offset = place[2, s]
        group = jnp.where(offset == 0, 0, jnp.where(offset == toward, 1, 2))

        @pl.when(jnp.logical_or(group != 2, inside))
        def _():
            r = pl.ds(pl.multiple_of(place[0, s] * tile, tile), tile)
            c = pl.ds(pl.multiple_of((group * tile_rows + place[1, s]) * tile, tile), tile)
            window[r, c] += tiles[s].astype(F32)

        return carry

    lax.fori_loop(0, tiles.shape[0], add, 0)
    near[...] = window[:, :rows].astype(BF)
    pair[...] = window[:, rows : 2 * rows].astype(BF)
    far[...] = window[:, 2 * rows :].astype(BF)
    limit = column(reach[...], 128)
    for g in range(cols.shape[1] // 128):
        here = slice(g * 128, (g + 1) * 128)
        lane = (lax.broadcasted_iota(jnp.int32, (rows, 128), 1) + g * 128).astype(F32)
        masked[:, here] = jnp.where(lane < limit, cols[:, here].astype(F32), 0.0).astype(BF)
    own[...] = mm(near[...], cells[...])


def near_kernel(near, cells, out):
    out[...] = mm(near[...], cells[...])


def sum_kernel(total, pair, cells, masked, mine, theirs, out, heads, *, head_dev):
    whole_heads(mine, theirs, heads, head_dev)
    out[...] = total[...] + mm(pair[...], cells[...]) + mm(masked[...], heads[...])


def fold_kernel(keep, arrived, kept, send):
    half = kept.shape[0]
    kept[...] = keep[:half] + arrived[:half].astype(F32)
    send[...] = (keep[half:] + arrived[half:].astype(F32)).astype(BF)


def join_kernel(*refs):
    size = refs[0].shape[0]
    for k, ref in enumerate(refs[:-1]):
        refs[-1][k * size : (k + 1) * size] = ref[...]


def whole_heads(mine, theirs, heads, head_dev):
    if not head_dev:
        heads[...] = mine[...]
        return
    pair, parity = lax.axis_index("rows") // 2, lax.axis_index("rows") % 2
    for n, k in enumerate(xor_order(mine.shape[0] // head_dev)):
        here = slice(n * head_dev, (n + 1) * head_dev)
        a = pl.multiple_of((2 * (pair ^ k) + parity) * head_dev, head_dev)
        b = pl.multiple_of((2 * (pair ^ k) + 1 - parity) * head_dev, head_dev)
        heads[pl.ds(a, head_dev)] = mine[here]
        heads[pl.ds(b, head_dev)] = theirs[here]


def first_sum_kernel(total, far, other, *refs):
    parts, out = refs[:-1], refs[-1]
    rows = total.shape[0]
    out[:rows] = (total[...] + mm(far[...], other[...])).astype(BF)
    if parts:
        extra = parts[0][...]
        for part in parts[1:]:
            extra = extra + part[...].astype(F32)
        out[rows:] = extra.astype(BF)


def last_sum_kernel(total, far, other, scale, out):
    out[...] = jnp.maximum((total[...] + mm(far[...], other[...])) * scale[...], 0.0)


def feature_rows(k, width):
    return pl.ds(pl.multiple_of((lax.axis_index("feat") ^ k) * width, width), width)


def mix_begin_kernel(*refs, early):
    half = (len(refs) - early) // 2
    pieces, shards, outs = refs[:early], refs[early : early + half], refs[early + half :]
    for shard, out in zip(shards, outs):
        total = None
        for k, piece in enumerate(pieces):
            term = mm(piece[...], shard[feature_rows(k, out.shape[1])])
            total = term if total is None else total + term
        out[...] = total


def mix_end_kernel(*refs, early, order, head_dev):
    pieces, refs = refs[:early], refs[early:]
    shards, refs = refs[: 2 * early], refs[2 * early :]
    begun, refs = refs[: 2 * early], refs[2 * early :]
    weights, band_scale, head_scale, *outs, scale = refs
    band, width = band_scale.shape
    scale[:band] = band_scale[...]
    if head_dev:
        scale[band:] = head_scale[...]
    result = None
    for n, (j, shard) in enumerate(zip(order, shards)):
        total = begun[n][...]
        for k, piece in enumerate(pieces):
            total = total + mm(piece[...], shard[feature_rows(early + k, width)])
        state = jnp.maximum(total * scale[...], 0.0).astype(BF)
        term = mm(state, weights[1, feature_rows(j, width)])
        result = term if result is None else result + term
    outs[0][...] = result[:band].astype(BF)
    if head_dev:
        outs[1][...] = result[band:].astype(BF)


def scale_kernel(degree, head_degree, scale, head_scale, all_scales):
    size = head_scale.shape[0]
    scale[...] = lax.rsqrt(column(degree[...], scale.shape[1]))
    all_scales[...] = lax.rsqrt(column(head_degree[...], scale.shape[1]))
    head_scale[...] = all_scales[pl.ds(pl.multiple_of(lax.axis_index("rows") * size, size), size)]


def wide_scale_kernel(degree, scale):
    scale[...] = lax.rsqrt(column(degree[...], scale.shape[1]))


def head_out_kernel(own, *refs):
    arrived, (scale, out) = refs[:-2], refs[-2:]
    total = own[...]
    for ref in arrived:
        total = total + ref[...].astype(F32)
    out[...] = jnp.maximum(total * scale[...], 0.0)


def body(
    band_feats,
    head_feats,
    mix_weights,
    tile_place,
    tile_vals,
    arrow_cols,
    arrow_reach,
    arrow_rows,
    band_degree,
    head_degree,
):
    rows_dev, width = band_feats.shape
    head_dev = head_feats.shape[0]
    heads = arrow_cols.shape[1]
    blocks = lax.axis_size("rows")
    pairs = blocks // 2
    top_bit = lax.axis_size("feat") // 2
    low_bits = [1 << n for n in reversed(range(top_bit.bit_length() - 1))]
    reach = arrow_reach[None, :]
    size = head_dev if pairs <= 4 and head_dev % 16 == 0 else 0
    part_rows = heads // 2 if size else heads
    part_scratch = pltpu.VMEM((heads, width), F32)
    head_scratch = pltpu.VMEM((heads, width), BF)
    band_sum = [((rows_dev, width), F32)]
    cells_shape = ((rows_dev, width), BF)
    head_sum = ((head_dev, width), F32)
    keep_shapes = [((part_rows, width), F32), ((part_rows, width), BF)]
    sum_up = functools.partial(sum_kernel, head_dev=size)

    def partial_sums(name, cells, *head):
        outs = [(h.shape, BF) for h in head] + keep_shapes
        add_up = functools.partial(partial_kernel, head_dev=size)
        return local(name, add_up, outs, (), (arrow_rows, cells, *head), [part_scratch])

    def gather_heads(name, own, before):
        if not size:
            everyone = lax.all_gather(own, "rows", axis=0, tiled=True)
            return everyone, everyone, everyone
        mine, halfway = own, None
        bit = pairs // 2
        while bit:
            other = swap(mine, "rows", 2 * bit)
            rows = 2 * mine.shape[0]
            (mine,) = local(name, join_kernel, [((rows, width), BF)], (), (after(mine, before), other))
            halfway = mine if halfway is None else halfway
            bit //= 2
        return halfway, mine, swap(mine, "rows", 1)

    def scatter_heads(name, keep, send, before):
        if not size:
            return []
        bit = 1
        while bit <= pairs:
            arrived = swap(send, "rows", bit)
            if bit < pairs:
                rows = keep.shape[0] // 2
                outs = [((rows, width), F32), ((rows, width), BF)]
                keep, send = local(name, fold_kernel, outs, (), (after(keep, before), arrived))
            bit *= 2
        return [keep, arrived]

    (cells,) = local("cast", cast_kernel, [cells_shape], (), (band_feats,))
    pair_cells = swap(cells, "rows", 1)
    first = after(mix_weights, cells)[0]
    across = swap(first, "feat", top_bit)
    head_cells, keep, send = partial_sums("part1", cells, head_feats)
    first_part = keep
    near, pair, far, masked, total = local(
        "dense",
        functools.partial(dense_kernel, blocks=blocks),
        [((rows_dev, rows_dev), BF)] * 3 + [((rows_dev, heads), BF), ((rows_dev, width), F32)],
        (tile_place.T,),
        (tile_vals, arrow_cols, reach, after(cells, keep)),
        [pltpu.VMEM((rows_dev, 3 * rows_dev), F32)],
    )
    halfway, mine, theirs = gather_heads("join1", head_cells, total)
    far_cells = forward(after(pair_cells, total))
    parts = scatter_heads("fold1", keep, send, total)
    total = after(total, *parts[:1])
    (total,) = local(
        "sum1", sum_up, band_sum, (), (total, pair, pair_cells, masked, mine, theirs), [head_scratch]
    )
    tall = rows_dev + size
    (joined,) = local(
        "first", first_sum_kernel, [((tall, width), BF)], (), (total, far, far_cells, *parts)
    )

    opposite = swap(joined, "feat", top_bit)
    band_degree = after(band_degree, joined)
    if size:
        scale, head_scale = local(
            "scale",
            scale_kernel,
            band_sum + [head_sum],
            (),
            (band_degree[None, :], head_degree[None, :]),
            [pltpu.VMEM((heads, width), F32)],
        )
    else:
        (scale,) = local("scale", wide_scale_kernel, band_sum, (), (band_degree[None, :],))
        head_scale = lax.rsqrt(head_degree.astype(F32))[:, None] * jnp.ones((1, width), F32)
        head_scale = lax.dynamic_slice_in_dim(head_scale, lax.axis_index("rows") * head_dev, head_dev, 0)
    pieces = spread("feat", after(joined, scale), low_bits)
    early = len(pieces)
    pieces.update({k | top_bit: c for k, c in spread("feat", opposite, low_bits).items()})
    pieces = [pieces[k] for k in sorted(pieces)]
    shards = spread("feat", after(first, scale), low_bits)
    shards.update({k | top_bit: w for k, w in spread("feat", after(across, scale), low_bits).items()})
    order = [0, top_bit] + [k for k in sorted(shards) if k not in (0, top_bit)]
    begun = local(
        "begin",
        functools.partial(mix_begin_kernel, early=early),
        [((tall, width), F32)] * 2,
        (),
        (after(pieces[0], opposite), *pieces[1:early], shards[0], shards[top_bit]),
    )
    if len(order) > 2:
        begun += local(
            "mid",
            functools.partial(mix_begin_kernel, early=early),
            [((tall, width), F32)] * (len(order) - 2),
            (),
            (after(pieces[0], begun[0]), *pieces[1:early], *[shards[k] for k in order[2:]]),
        )
    cells, *head_x = local(
        "end",
        functools.partial(mix_end_kernel, early=early, order=order, head_dev=size),
        [cells_shape] + ([((size, width), BF)] if size else []),
        (),
        (*pieces[early:], *[shards[k] for k in order], *begun, mix_weights, scale, head_scale),
        [pltpu.VMEM((tall, width), F32)],
    )
    if not size:
        summed = lax.psum_scatter(first_part, "rows", scatter_dimension=0, tiled=True).astype(BF)
        summed = lax.all_gather(summed, "feat", axis=1, tiled=True)
        full = lax.all_gather(mix_weights[0], "feat", axis=1, tiled=True)
        head_state = jnp.maximum(mm(summed, full) * head_scale[:, :1], 0.0).astype(BF)
        head_x = [mm(head_state, mix_weights[1]).astype(BF)]

    keep, send = partial_sums("part2", cells)
    pair_cells = swap(after(cells, keep), "rows", 1)
    (total,) = local("near", near_kernel, band_sum, (), (after(near, keep), cells))
    halfway, mine, theirs = gather_heads("join2", after(head_x[0], keep), total)
    far_cells = forward(after(pair_cells, halfway))
    parts = scatter_heads("fold2", keep, send, mine)
    (total,) = local(
        "sum2", sum_up, band_sum, (), (after(total, *parts[:1]), pair, pair_cells, masked, mine, theirs), [head_scratch]
    )
    (band_out,) = local("last", last_sum_kernel, band_sum, (), (total, far, far_cells, scale))
    if size:
        own = after(parts[0], band_out)
        (head_out,) = local("headout", head_out_kernel, [head_sum], (), (own, *parts[1:], head_scale))
    else:
        head_out = jnp.maximum(lax.psum_scatter(keep, "rows", scatter_dimension=0, tiled=True) * head_scale, 0.0)
    return band_out, head_out


def solution(mesh):
    in_specs = (
        P("rows", "feat"),
        P("rows", "feat"),
        P(None, None, "feat"),
        P("rows", None),
        P("rows", None, None),
        P("rows", None),
        P("rows"),
        P(None, "rows"),
        P("rows"),
        P(),
    )
    out_specs = (P("rows", "feat"), P("rows", "feat"))
    return jax.shard_map(body, mesh=mesh, in_specs=in_specs, out_specs=out_specs, check_vma=False)
```

```python
import functools

import jax
import jax.numpy as jnp
from jax import lax
from jax.experimental import pallas as pl
from jax.experimental.pallas import tpu as pltpu
from jax.sharding import PartitionSpec as P

BF = jnp.bfloat16
F32 = jnp.float32
LIMIT = 16 * 1024 * 1024
WORK = {
    "cast": 1_000_000,
    "part1": 4_000_000_000,
    "dense": 1_000_000,
    "join1": 500_000_000,
    "fold1": 2_000_000_000,
    "sum1": 1_000_000,
    "first": 500_000_000,
    "scale": 500_000_000,
    "begin": 1_000_000_000,
    "mid": 500_000_000,
    "end": 500_000_000,
    "part2": 1_000_000,
    "near": 500_000_000,
    "join2": 500_000_000,
    "fold2": 1_000_000,
    "sum2": 500_000_000,
    "last": 500_000_000,
    "headout": 1_000_000,
    "collect": 500_000_000,
    "join3": 500_000_000,
    "headmix": 500_000_000,
}


def local(name, kernel, outs, scalars, args, scratch=()):
    vmem = pl.BlockSpec(memory_space=pltpu.VMEM)
    smem = pl.BlockSpec(memory_space=pltpu.SMEM)
    moved = sum(a.size * a.dtype.itemsize for a in args)
    return pl.pallas_call(
        kernel,
        out_shape=[jax.ShapeDtypeStruct(s, d) for s, d in outs],
        in_specs=[smem] * len(scalars) + [vmem] * len(args),
        out_specs=[vmem] * len(outs),
        scratch_shapes=list(scratch),
        cost_estimate=pl.CostEstimate(flops=WORK[name], bytes_accessed=moved, transcendentals=0),
        compiler_params=pltpu.CompilerParams(vmem_limit_bytes=LIMIT),
    )(*scalars, *args)


def mm(a, b):
    return jnp.dot(a, b, preferred_element_type=F32)


def swap(cells, axis, bit):
    count = lax.axis_size(axis)
    return lax.ppermute(cells, axis, [(i, i ^ bit) for i in range(count)])


def forward(cells):
    count = lax.axis_size("rows")
    pairs = []
    for i in range(count):
        if i % 2 == 0:
            pairs.append((i, i + 2 if i + 2 < count else i + 1))
        else:
            pairs.append((i, i - 2 if i > 1 else 0))
    return lax.ppermute(cells, "rows", pairs)


def spread(axis, cells, bits):
    pieces = {0: cells}
    for bit in bits:
        pieces.update({k | bit: swap(c, axis, bit) for k, c in list(pieces.items())})
    return pieces


def column(values, width):
    wide = jnp.broadcast_to(values.astype(F32), (128, values.shape[1]))
    tall = wide.T
    return jnp.concatenate([tall] * (width // 128), axis=1) if width > 128 else tall


def after(value, *others):
    return lax.optimization_barrier((value, *others))[0]


def xor_order(count):
    order = [0]
    bit = count // 2
    while bit:
        order += [k | bit for k in order]
        bit //= 2
    return order


def split_partial(part, keep, send, head_dev, bits):
    if not head_dev:
        keep[...] = part[...]
        send[...] = part[...].astype(BF)
        return
    half = len(bits) - 1
    for n in range(2 << half):
        owner = lax.axis_index("rows") ^ sum(bit for i, bit in enumerate(bits) if n >> (half - i) & 1)
        rows = part[pl.ds(pl.multiple_of(owner * head_dev, head_dev), head_dev)]
        if n < 1 << half:
            keep[n * head_dev : (n + 1) * head_dev] = rows
        else:
            n -= 1 << half
            send[n * head_dev : (n + 1) * head_dev] = rows.astype(BF)


def cast_kernel(cells, out):
    out[...] = cells[...].astype(BF)


def partial_kernel(rows, cells, *refs, head_dev, bits):
    keep, send, part = refs[-3:]
    if len(refs) > 3:
        refs[1][...] = refs[0][...].astype(BF)
    part[...] = mm(rows[...], cells[...])
    split_partial(part, keep, send, head_dev, bits)


def dense_kernel(place, tiles, cols, reach, cells, near, pair, far, masked, own, window, *, blocks):
    tile = tiles.shape[1]
    rows = window.shape[0]
    tile_rows = rows // tile
    parity = lax.axis_index("rows") % 2
    toward = 1 - 2 * parity
    inside = jnp.logical_and(lax.axis_index("rows") != 0, lax.axis_index("rows") != blocks - 1)
    window[...] = jnp.zeros_like(window)

    def add(s, carry):
        offset = place[2, s]
        group = jnp.where(offset == 0, 0, jnp.where(offset == toward, 1, 2))

        @pl.when(jnp.logical_or(group != 2, inside))
        def _():
            r = pl.ds(pl.multiple_of(place[0, s] * tile, tile), tile)
            c = pl.ds(pl.multiple_of((group * tile_rows + place[1, s]) * tile, tile), tile)
            window[r, c] += tiles[s].astype(F32)

        return carry

    lax.fori_loop(0, tiles.shape[0], add, 0)
    near[...] = window[:, :rows].astype(BF)
    pair[...] = window[:, rows : 2 * rows].astype(BF)
    far[...] = window[:, 2 * rows :].astype(BF)
    limit = column(reach[...], 128)
    for g in range(cols.shape[1] // 128):
        here = slice(g * 128, (g + 1) * 128)
        lane = (lax.broadcasted_iota(jnp.int32, (rows, 128), 1) + g * 128).astype(F32)
        masked[:, here] = jnp.where(lane < limit, cols[:, here].astype(F32), 0.0).astype(BF)
    own[...] = mm(near[...], cells[...])


def near_kernel(near, cells, out):
    out[...] = mm(near[...], cells[...])


def sum_kernel(total, pair, cells, masked, mine, theirs, out, heads, *, head_dev):
    whole_heads(mine, theirs, heads, head_dev)
    out[...] = total[...] + mm(pair[...], cells[...]) + mm(masked[...], heads[...])


def fold_kernel(keep, arrived, kept, send):
    half = kept.shape[0]
    kept[...] = keep[:half] + arrived[:half].astype(F32)
    send[...] = (keep[half:] + arrived[half:].astype(F32)).astype(BF)


def join_kernel(*refs):
    size = refs[0].shape[0]
    for k, ref in enumerate(refs[:-1]):
        refs[-1][k * size : (k + 1) * size] = ref[...]


def whole_heads(mine, theirs, heads, head_dev):
    if not head_dev:
        heads[...] = mine[...]
        return
    pair, parity = lax.axis_index("rows") // 2, lax.axis_index("rows") % 2
    for n, k in enumerate(xor_order(mine.shape[0] // head_dev)):
        here = slice(n * head_dev, (n + 1) * head_dev)
        a = pl.multiple_of((2 * (pair ^ k) + parity) * head_dev, head_dev)
        b = pl.multiple_of((2 * (pair ^ k) + 1 - parity) * head_dev, head_dev)
        heads[pl.ds(a, head_dev)] = mine[here]
        heads[pl.ds(b, head_dev)] = theirs[here]


def first_sum_kernel(total, far, other, *refs):
    parts, out = refs[:-1], refs[-1]
    rows = total.shape[0]
    out[:rows] = (total[...] + mm(far[...], other[...])).astype(BF)
    if parts:
        extra = parts[0][...]
        for part in parts[1:]:
            extra = extra + part[...].astype(F32)
        out[rows:] = extra.astype(BF)


def last_sum_kernel(total, far, other, scale, out):
    out[...] = jnp.maximum((total[...] + mm(far[...], other[...])) * scale[...], 0.0)


def feature_rows(k, width):
    return pl.ds(pl.multiple_of((lax.axis_index("feat") ^ k) * width, width), width)


def mix_begin_kernel(*refs, early):
    half = (len(refs) - early) // 2
    pieces, shards, outs = refs[:early], refs[early : early + half], refs[early + half :]
    for shard, out in zip(shards, outs):
        total = None
        for k, piece in enumerate(pieces):
            term = mm(piece[...], shard[feature_rows(k, out.shape[1])])
            total = term if total is None else total + term
        out[...] = total


def mix_end_kernel(*refs, early, order, head_dev):
    pieces, refs = refs[:early], refs[early:]
    shards, refs = refs[: 2 * early], refs[2 * early :]
    begun, refs = refs[: 2 * early], refs[2 * early :]
    weights, band_scale, head_scale, *outs, scale = refs
    band, width = band_scale.shape
    scale[:band] = band_scale[...]
    if head_dev:
        scale[band:] = head_scale[...]
    result = None
    for n, (j, shard) in enumerate(zip(order, shards)):
        total = begun[n][...]
        for k, piece in enumerate(pieces):
            total = total + mm(piece[...], shard[feature_rows(early + k, width)])
        state = jnp.maximum(total * scale[...], 0.0).astype(BF)
        term = mm(state, weights[1, feature_rows(j, width)])
        result = term if result is None else result + term
    outs[0][...] = result[:band].astype(BF)
    if head_dev:
        outs[1][...] = result[band:].astype(BF)


def scale_kernel(degree, head_degree, scale, head_scale, all_scales):
    size = head_scale.shape[0]
    scale[...] = lax.rsqrt(column(degree[...], scale.shape[1]))
    all_scales[...] = lax.rsqrt(column(head_degree[...], scale.shape[1]))
    head_scale[...] = all_scales[pl.ds(pl.multiple_of(lax.axis_index("rows") * size, size), size)]


def wide_scale_kernel(degree, scale):
    scale[...] = lax.rsqrt(column(degree[...], scale.shape[1]))


def head_out_kernel(own, *refs):
    arrived, (scale, out) = refs[:-2], refs[-2:]
    total = own[...]
    for ref in arrived:
        total = total + ref[...].astype(F32)
    out[...] = jnp.maximum(total * scale[...], 0.0)


def body(
    band_feats,
    head_feats,
    mix_weights,
    tile_place,
    tile_vals,
    arrow_cols,
    arrow_reach,
    arrow_rows,
    band_degree,
    head_degree,
):
    rows_dev, width = band_feats.shape
    head_dev = head_feats.shape[0]
    heads = arrow_cols.shape[1]
    blocks = lax.axis_size("rows")
    pairs = blocks // 2
    top_bit = lax.axis_size("feat") // 2
    low_bits = [1 << n for n in reversed(range(top_bit.bit_length() - 1))]
    reach = arrow_reach[None, :]
    size = head_dev if pairs <= 4 and head_dev % 16 == 0 else 0
    part_rows = heads // 2 if size else heads
    index_bits = [1 << n for n in range(blocks.bit_length() - 1)]
    bits, last_bits = [*index_bits[1:2], index_bits[0], *index_bits[2:]], [*index_bits[1:2], index_bits[0], *index_bits[2:]]
    part_scratch = pltpu.VMEM((heads, width), F32)
    head_scratch = pltpu.VMEM((heads, width), BF)
    band_sum = [((rows_dev, width), F32)]
    cells_shape = ((rows_dev, width), BF)
    head_sum = ((head_dev, width), F32)
    keep_shapes = [((part_rows, width), F32), ((part_rows, width), BF)]
    sum_up = functools.partial(sum_kernel, head_dev=size)

    def partial_sums(name, bits, cells, *head):
        outs = [(h.shape, BF) for h in head] + keep_shapes
        add_up = functools.partial(partial_kernel, head_dev=size, bits=bits)
        return local(name, add_up, outs, (), (arrow_rows, cells, *head), [part_scratch])

    def join(name, mine, other, before):
        shape = ((2 * mine.shape[0], width), BF)
        return local(name, join_kernel, [shape], (), (after(mine, before), other))[0]

    def fold(name, keep, arrived, before):
        rows = keep.shape[0] // 2
        outs = [((rows, width), F32), ((rows, width), BF)]
        return local(name, fold_kernel, outs, (), (after(keep, before), arrived))

    def exchange(joining, folding, own, keep, send, before, bits, turns, pause, between):
        if not size:
            between(before)
            everyone = lax.all_gather(own, "rows", axis=0, tiled=True)
            return everyone, everyone, []
        mine, gathers, halves = own, list(index_bits[:0:-1]), list(bits)
        other = swap(mine, "rows", gathers.pop(0))
        arrived = swap(send, "rows", halves.pop(0))
        for n, turn in enumerate(turns):
            if n == pause:
                before = between(before)
            if turn == "j":
                mine = before = join(joining, mine, other, before)
                other = swap(mine, "rows", gathers.pop(0) if gathers else 1)
            else:
                keep, send = fold(folding, keep, arrived, before)
                before = keep
                arrived = swap(send, "rows", halves.pop(0))
        if pause == len(turns):
            between(before)
        return mine, other, [keep, arrived]

    (cells,) = local("cast", cast_kernel, [cells_shape], (), (band_feats,))
    pair_cells = swap(cells, "rows", 1)
    first = after(mix_weights, cells)[0]
    across = swap(first, "feat", top_bit)
    head_cells, keep, send = partial_sums("part1", bits, cells, head_feats)
    first_part = keep
    laid = []

    def lay_out(before):
        outs = [((rows_dev, rows_dev), BF)] * 3 + [((rows_dev, heads), BF)] + band_sum
        args = (tile_vals, arrow_cols, reach, after(cells, before))
        scratch = [pltpu.VMEM((rows_dev, 3 * rows_dev), F32)]
        kernel = functools.partial(dense_kernel, blocks=blocks)
        laid.extend(local("dense", kernel, outs, (tile_place.T,), args, scratch))
        return laid[-1]

    mine, theirs, parts = exchange(
        "join1", "fold1", head_cells, keep, send, keep, bits, "jfjf", 3, lay_out
    )
    near, pair, far, masked, total = laid
    far_cells = forward(after(pair_cells, first_part))
    (total,) = local(
        "sum1", sum_up, band_sum, (), (total, pair, pair_cells, masked, mine, theirs), [head_scratch]
    )
    tall = rows_dev + size
    (joined,) = local(
        "first", first_sum_kernel, [((tall, width), BF)], (), (total, far, far_cells, *parts)
    )

    opposite = swap(joined, "feat", top_bit)
    band_degree = after(band_degree, joined)
    if size:
        scale, head_scale = local(
            "scale",
            scale_kernel,
            band_sum + [head_sum],
            (),
            (band_degree[None, :], head_degree[None, :]),
            [pltpu.VMEM((heads, width), F32)],
        )
    else:
        (scale,) = local("scale", wide_scale_kernel, band_sum, (), (band_degree[None, :],))
        head_scale = lax.rsqrt(head_degree.astype(F32))[:, None] * jnp.ones((1, width), F32)
        head_scale = lax.dynamic_slice_in_dim(head_scale, lax.axis_index("rows") * head_dev, head_dev, 0)
    pieces = spread("feat", after(joined, scale), low_bits)
    early = len(pieces)
    pieces.update({k | top_bit: c for k, c in spread("feat", opposite, low_bits).items()})
    pieces = [pieces[k] for k in sorted(pieces)]
    shards = spread("feat", after(first, scale), low_bits)
    shards.update({k | top_bit: w for k, w in spread("feat", after(across, scale), low_bits).items()})
    order = [0, top_bit] + [k for k in sorted(shards) if k not in (0, top_bit)]
    begun = local(
        "begin",
        functools.partial(mix_begin_kernel, early=early),
        [((tall, width), F32)] * 2,
        (),
        (after(pieces[0], opposite), *pieces[1:early], shards[0], shards[top_bit]),
    )
    if len(order) > 2:
        begun += local(
            "mid",
            functools.partial(mix_begin_kernel, early=early),
            [((tall, width), F32)] * (len(order) - 2),
            (),
            (after(pieces[0], begun[0]), *pieces[1:early], *[shards[k] for k in order[2:]]),
        )
    cells, *head_x = local(
        "end",
        functools.partial(mix_end_kernel, early=early, order=order, head_dev=size),
        [cells_shape] + ([((size, width), BF)] if size else []),
        (),
        (*pieces[early:], *[shards[k] for k in order], *begun, mix_weights, scale, head_scale),
        [pltpu.VMEM((tall, width), F32)],
    )
    if not size:
        summed = lax.psum_scatter(first_part, "rows", scatter_dimension=0, tiled=True).astype(BF)
        summed = lax.all_gather(summed, "feat", axis=1, tiled=True)
        full = lax.all_gather(mix_weights[0], "feat", axis=1, tiled=True)
        head_state = jnp.maximum(mm(summed, full) * head_scale[:, :1], 0.0).astype(BF)
        head_x = [mm(head_state, mix_weights[1]).astype(BF)]

    pair_cells = swap(cells, "rows", 1)
    keep, send = partial_sums("part2", last_bits, cells)
    sums = []

    def multiply(before):
        sums.extend(local("near", near_kernel, band_sum, (), (after(near, before), cells)))
        return sums[-1]

    mine, theirs, parts = exchange(
        "join2", "fold2", after(head_x[0], keep), keep, send, keep, last_bits, "fjfj", 0, multiply
    )
    (total,) = sums
    far_cells = forward(after(pair_cells, total))
    (total,) = local(
        "sum2", sum_up, band_sum, (), (after(total, *parts[:1]), pair, pair_cells, masked, mine, theirs), [head_scratch]
    )
    (band_out,) = local("last", last_sum_kernel, band_sum, (), (total, far, far_cells, scale))
    if size:
        own = after(parts[0], band_out)
        (head_out,) = local("headout", head_out_kernel, [head_sum], (), (own, *parts[1:], head_scale))
    else:
        head_out = jnp.maximum(lax.psum_scatter(keep, "rows", scatter_dimension=0, tiled=True) * head_scale, 0.0)
    return band_out, head_out


def solution(mesh):
    in_specs = (
        P("rows", "feat"),
        P("rows", "feat"),
        P(None, None, "feat"),
        P("rows", None),
        P("rows", None, None),
        P("rows", None),
        P("rows"),
        P(None, "rows"),
        P("rows"),
        P(),
    )
    out_specs = (P("rows", "feat"), P("rows", "feat"))
    return jax.shard_map(body, mesh=mesh, in_specs=in_specs, out_specs=out_specs, check_vma=False)
```

```python
import functools

import jax
import jax.numpy as jnp
from jax import lax
from jax.experimental import pallas as pl
from jax.experimental.pallas import tpu as pltpu
from jax.sharding import PartitionSpec as P

BF = jnp.bfloat16
F32 = jnp.float32
LIMIT = 16 * 1024 * 1024
WORK = {
    "cast": 1_000_000,
    "part1": 2_000_000_000,
    "dense": 1_000_000,
    "join1": 200_000_000,
    "fold1": 2_000_000_000,
    "sum1": 1_000_000,
    "first": 1_000_000,
    "scale": 500_000_000,
    "begin": 1_000_000,
    "mid": 200_000_000,
    "end": 500_000_000,
    "part2": 1_000_000,
    "near": 500_000_000,
    "join2": 10_000,
    "fold2": 4_000_000_000,
    "sum2": 2_000_000_000,
    "last": 500_000_000,
    "collect": 500_000_000,
    "join3": 500_000_000,
    "headmix": 500_000_000,
}


def local(name, kernel, outs, scalars, args, scratch=()):
    vmem = pl.BlockSpec(memory_space=pltpu.VMEM)
    smem = pl.BlockSpec(memory_space=pltpu.SMEM)
    moved = sum(a.size * a.dtype.itemsize for a in args)
    return pl.pallas_call(
        kernel,
        out_shape=[jax.ShapeDtypeStruct(s, d) for s, d in outs],
        in_specs=[smem] * len(scalars) + [vmem] * len(args),
        out_specs=[vmem] * len(outs),
        scratch_shapes=list(scratch),
        cost_estimate=pl.CostEstimate(flops=WORK[name], bytes_accessed=moved, transcendentals=0),
        compiler_params=pltpu.CompilerParams(vmem_limit_bytes=LIMIT),
    )(*scalars, *args)


def mm(a, b):
    return jnp.dot(a, b, preferred_element_type=F32)


def swap(cells, axis, bit):
    count = lax.axis_size(axis)
    return lax.ppermute(cells, axis, [(i, i ^ bit) for i in range(count)])


def forward(cells):
    count = lax.axis_size("rows")
    pairs = []
    for i in range(count):
        if i % 2 == 0:
            pairs.append((i, i + 2 if i + 2 < count else i + 1))
        else:
            pairs.append((i, i - 2 if i > 1 else 0))
    return lax.ppermute(cells, "rows", pairs)


def spread(axis, cells, bits):
    pieces = {0: cells}
    for bit in bits:
        pieces.update({k | bit: swap(c, axis, bit) for k, c in list(pieces.items())})
    return pieces


def column(values, width):
    wide = jnp.broadcast_to(values.astype(F32), (128, values.shape[1]))
    tall = wide.T
    return jnp.concatenate([tall] * (width // 128), axis=1) if width > 128 else tall


def after(value, *others):
    return lax.optimization_barrier((value, *others))[0]


def xor_order(count):
    order = [0]
    bit = count // 2
    while bit:
        order += [k | bit for k in order]
        bit //= 2
    return order


def split_partial(part, keep, send, head_dev, bits):
    if not head_dev:
        keep[...] = part[...]
        send[...] = part[...].astype(BF)
        return
    half = len(bits) - 1
    for n in range(2 << half):
        owner = lax.axis_index("rows") ^ sum(bit for i, bit in enumerate(bits) if n >> (half - i) & 1)
        rows = part[pl.ds(pl.multiple_of(owner * head_dev, head_dev), head_dev)]
        if n < 1 << half:
            keep[n * head_dev : (n + 1) * head_dev] = rows
        else:
            n -= 1 << half
            send[n * head_dev : (n + 1) * head_dev] = rows.astype(BF)


def cast_kernel(cells, out):
    out[...] = cells[...].astype(BF)


def partial_kernel(rows, cells, *refs, head_dev, bits):
    keep, send, part = refs[-3:]
    if len(refs) > 3:
        refs[1][...] = refs[0][...].astype(BF)
    part[...] = mm(rows[...], cells[...])
    split_partial(part, keep, send, head_dev, bits)


def dense_kernel(place, tiles, cols, reach, cells, near, pair, far, masked, own, window, *, blocks):
    tile = tiles.shape[1]
    rows = window.shape[0]
    tile_rows = rows // tile
    parity = lax.axis_index("rows") % 2
    toward = 1 - 2 * parity
    inside = jnp.logical_and(lax.axis_index("rows") != 0, lax.axis_index("rows") != blocks - 1)
    window[...] = jnp.zeros_like(window)

    def add(s, carry):
        offset = place[2, s]
        group = jnp.where(offset == 0, 0, jnp.where(offset == toward, 1, 2))

        @pl.when(jnp.logical_or(group != 2, inside))
        def _():
            r = pl.ds(pl.multiple_of(place[0, s] * tile, tile), tile)
            c = pl.ds(pl.multiple_of((group * tile_rows + place[1, s]) * tile, tile), tile)
            window[r, c] += tiles[s].astype(F32)

        return carry

    lax.fori_loop(0, tiles.shape[0], add, 0)
    near[...] = window[:, :rows].astype(BF)
    pair[...] = window[:, rows : 2 * rows].astype(BF)
    far[...] = window[:, 2 * rows :].astype(BF)
    limit = column(reach[...], 128)
    for g in range(cols.shape[1] // 128):
        here = slice(g * 128, (g + 1) * 128)
        lane = (lax.broadcasted_iota(jnp.int32, (rows, 128), 1) + g * 128).astype(F32)
        masked[:, here] = jnp.where(lane < limit, cols[:, here].astype(F32), 0.0).astype(BF)
    own[...] = mm(near[...], cells[...])


def near_kernel(near, cells, out):
    out[...] = mm(near[...], cells[...])


def sum_kernel(total, pair, cells, masked, mine, theirs, out, heads, *, head_dev):
    whole_heads(mine, theirs, heads, head_dev)
    out[...] = total[...] + mm(pair[...], cells[...]) + mm(masked[...], heads[...])


def fold_kernel(keep, arrived, kept, send):
    half = kept.shape[0]
    kept[...] = keep[:half] + arrived[:half].astype(F32)
    send[...] = (keep[half:] + arrived[half:].astype(F32)).astype(BF)


def join_kernel(*refs):
    size = refs[0].shape[0]
    for k, ref in enumerate(refs[:-1]):
        refs[-1][k * size : (k + 1) * size] = ref[...]


def whole_heads(mine, theirs, heads, head_dev):
    if not head_dev:
        heads[...] = mine[...]
        return
    pair, parity = lax.axis_index("rows") // 2, lax.axis_index("rows") % 2
    for n, k in enumerate(xor_order(mine.shape[0] // head_dev)):
        here = slice(n * head_dev, (n + 1) * head_dev)
        a = pl.multiple_of((2 * (pair ^ k) + parity) * head_dev, head_dev)
        b = pl.multiple_of((2 * (pair ^ k) + 1 - parity) * head_dev, head_dev)
        heads[pl.ds(a, head_dev)] = mine[here]
        heads[pl.ds(b, head_dev)] = theirs[here]


def first_sum_kernel(total, far, other, *refs):
    parts, out = refs[:-1], refs[-1]
    rows = total.shape[0]
    out[:rows] = (total[...] + mm(far[...], other[...])).astype(BF)
    if parts:
        extra = parts[0][...]
        for part in parts[1:]:
            extra = extra + part[...].astype(F32)
        out[rows:] = extra.astype(BF)


def add_kernel(total, pair, cells, out):
    out[...] = total[...] + mm(pair[...], cells[...])


def last_kernel(total, far, other, masked, mine, theirs, scale, *refs, head_dev):
    if head_dev:
        own, arrived, head_scale, out, head_out, heads = refs
        head_out[...] = jnp.maximum((own[...] + arrived[...].astype(F32)) * head_scale[...], 0.0)
    else:
        out, heads = refs
    whole_heads(mine, theirs, heads, head_dev)
    band = total[...] + mm(far[...], other[...]) + mm(masked[...], heads[...])
    out[...] = jnp.maximum(band * scale[...], 0.0)


def feature_rows(k, width):
    return pl.ds(pl.multiple_of((lax.axis_index("feat") ^ k) * width, width), width)


def mix_begin_kernel(*refs, early):
    half = (len(refs) - early) // 2
    pieces, shards, outs = refs[:early], refs[early : early + half], refs[early + half :]
    for shard, out in zip(shards, outs):
        total = None
        for k, piece in enumerate(pieces):
            term = mm(piece[...], shard[feature_rows(k, out.shape[1])])
            total = term if total is None else total + term
        out[...] = total


def mix_end_kernel(*refs, early, order, head_dev):
    pieces, refs = refs[:early], refs[early:]
    shards, refs = refs[: 2 * early], refs[2 * early :]
    begun, refs = refs[: 2 * early], refs[2 * early :]
    weights, band_scale, head_scale, *outs, scale = refs
    band, width = band_scale.shape
    scale[:band] = band_scale[...]
    if head_dev:
        scale[band:] = head_scale[...]
    result = None
    for n, (j, shard) in enumerate(zip(order, shards)):
        total = begun[n][...]
        for k, piece in enumerate(pieces):
            total = total + mm(piece[...], shard[feature_rows(early + k, width)])
        state = jnp.maximum(total * scale[...], 0.0).astype(BF)
        term = mm(state, weights[1, feature_rows(j, width)])
        result = term if result is None else result + term
    outs[0][...] = result[:band].astype(BF)
    if head_dev:
        outs[1][...] = result[band:].astype(BF)


def scale_kernel(degree, head_degree, scale, head_scale, all_scales):
    size = head_scale.shape[0]
    scale[...] = lax.rsqrt(column(degree[...], scale.shape[1]))
    all_scales[...] = lax.rsqrt(column(head_degree[...], scale.shape[1]))
    head_scale[...] = all_scales[pl.ds(pl.multiple_of(lax.axis_index("rows") * size, size), size)]


def wide_scale_kernel(degree, scale):
    scale[...] = lax.rsqrt(column(degree[...], scale.shape[1]))


def body(
    band_feats,
    head_feats,
    mix_weights,
    tile_place,
    tile_vals,
    arrow_cols,
    arrow_reach,
    arrow_rows,
    band_degree,
    head_degree,
):
    rows_dev, width = band_feats.shape
    head_dev = head_feats.shape[0]
    heads = arrow_cols.shape[1]
    blocks = lax.axis_size("rows")
    pairs = blocks // 2
    top_bit = lax.axis_size("feat") // 2
    low_bits = [1 << n for n in reversed(range(top_bit.bit_length() - 1))]
    reach = arrow_reach[None, :]
    size = head_dev if pairs <= 4 and head_dev % 16 == 0 else 0
    part_rows = heads // 2 if size else heads
    index_bits = [1 << n for n in range(blocks.bit_length() - 1)]
    bits, last_bits = [*index_bits[1:2], index_bits[0], *index_bits[2:]], [*index_bits[1:2], index_bits[0], *index_bits[2:]]
    part_scratch = pltpu.VMEM((heads, width), F32)
    head_scratch = pltpu.VMEM((heads, width), BF)
    band_sum = [((rows_dev, width), F32)]
    cells_shape = ((rows_dev, width), BF)
    head_sum = ((head_dev, width), F32)
    keep_shapes = [((part_rows, width), F32), ((part_rows, width), BF)]
    sum_up = functools.partial(sum_kernel, head_dev=size)

    def partial_sums(name, bits, cells, *head):
        outs = [(h.shape, BF) for h in head] + keep_shapes
        add_up = functools.partial(partial_kernel, head_dev=size, bits=bits)
        return local(name, add_up, outs, (), (arrow_rows, cells, *head), [part_scratch])

    def join(name, mine, other, before):
        shape = ((2 * mine.shape[0], width), BF)
        return local(name, join_kernel, [shape], (), (after(mine, before), other))[0]

    def fold(name, keep, arrived, before):
        rows = keep.shape[0] // 2
        outs = [((rows, width), F32), ((rows, width), BF)]
        return local(name, fold_kernel, outs, (), (after(keep, before), arrived))

    def exchange(joining, folding, own, keep, send, before, bits, turns, pause, between):
        if not size:
            between(before)
            everyone = lax.all_gather(own, "rows", axis=0, tiled=True)
            return everyone, everyone, []
        mine, gathers, halves = own, list(index_bits[:0:-1]), list(bits)
        other = swap(mine, "rows", gathers.pop(0))
        arrived = swap(send, "rows", halves.pop(0))
        for n, turn in enumerate(turns):
            if n == pause:
                before = between(before)
            if turn == "j":
                mine = before = join(joining, mine, other, before)
                other = swap(mine, "rows", gathers.pop(0) if gathers else 1)
            else:
                keep, send = fold(folding, keep, arrived, before)
                before = keep
                arrived = swap(send, "rows", halves.pop(0))
        if pause == len(turns):
            between(before)
        return mine, other, [keep, arrived]

    (cells,) = local("cast", cast_kernel, [cells_shape], (), (band_feats,))
    pair_cells = swap(cells, "rows", 1)
    first = after(mix_weights, cells)[0]
    across = swap(first, "feat", top_bit)
    head_cells, keep, send = partial_sums("part1", bits, cells, head_feats)
    first_part = keep
    laid = []

    def lay_out(before):
        outs = [((rows_dev, rows_dev), BF)] * 3 + [((rows_dev, heads), BF)] + band_sum
        args = (tile_vals, arrow_cols, reach, after(cells, before))
        scratch = [pltpu.VMEM((rows_dev, 3 * rows_dev), F32)]
        kernel = functools.partial(dense_kernel, blocks=blocks)
        laid.extend(local("dense", kernel, outs, (tile_place.T,), args, scratch))
        return laid[-1]

    mine, theirs, parts = exchange(
        "join1", "fold1", head_cells, keep, send, keep, bits, "jfjf", 3, lay_out
    )
    near, pair, far, masked, total = laid
    far_cells = forward(after(pair_cells, first_part))
    (total,) = local(
        "sum1", sum_up, band_sum, (), (total, pair, pair_cells, masked, mine, theirs), [head_scratch]
    )
    tall = rows_dev + size
    (joined,) = local(
        "first", first_sum_kernel, [((tall, width), BF)], (), (total, far, far_cells, *parts)
    )

    opposite = swap(joined, "feat", top_bit)
    band_degree = after(band_degree, joined)
    if size:
        scale, head_scale = local(
            "scale",
            scale_kernel,
            band_sum + [head_sum],
            (),
            (band_degree[None, :], head_degree[None, :]),
            [pltpu.VMEM((heads, width), F32)],
        )
    else:
        (scale,) = local("scale", wide_scale_kernel, band_sum, (), (band_degree[None, :],))
        head_scale = lax.rsqrt(head_degree.astype(F32))[:, None] * jnp.ones((1, width), F32)
        head_scale = lax.dynamic_slice_in_dim(head_scale, lax.axis_index("rows") * head_dev, head_dev, 0)
    pieces = spread("feat", after(joined, scale), low_bits)
    early = len(pieces)
    pieces.update({k | top_bit: c for k, c in spread("feat", opposite, low_bits).items()})
    pieces = [pieces[k] for k in sorted(pieces)]
    shards = spread("feat", after(first, scale), low_bits)
    shards.update({k | top_bit: w for k, w in spread("feat", after(across, scale), low_bits).items()})
    order = [0, top_bit] + [k for k in sorted(shards) if k not in (0, top_bit)]
    begun = local(
        "begin",
        functools.partial(mix_begin_kernel, early=early),
        [((tall, width), F32)] * 2,
        (),
        (after(pieces[0], opposite), *pieces[1:early], shards[0], shards[top_bit]),
    )
    if len(order) > 2:
        begun += local(
            "mid",
            functools.partial(mix_begin_kernel, early=early),
            [((tall, width), F32)] * (len(order) - 2),
            (),
            (after(pieces[0], begun[0]), *pieces[1:early], *[shards[k] for k in order[2:]]),
        )
    cells, *head_x = local(
        "end",
        functools.partial(mix_end_kernel, early=early, order=order, head_dev=size),
        [cells_shape] + ([((size, width), BF)] if size else []),
        (),
        (*pieces[early:], *[shards[k] for k in order], *begun, mix_weights, scale, head_scale),
        [pltpu.VMEM((tall, width), F32)],
    )
    if not size:
        summed = lax.psum_scatter(first_part, "rows", scatter_dimension=0, tiled=True).astype(BF)
        summed = lax.all_gather(summed, "feat", axis=1, tiled=True)
        full = lax.all_gather(mix_weights[0], "feat", axis=1, tiled=True)
        head_state = jnp.maximum(mm(summed, full) * head_scale[:, :1], 0.0).astype(BF)
        head_x = [mm(head_state, mix_weights[1]).astype(BF)]

    keep, send = partial_sums("part2", last_bits, cells)
    pair_cells = swap(after(cells, keep), "rows", 1)
    sums = []

    def multiply(before):
        sums.extend(local("near", near_kernel, band_sum, (), (after(near, before), cells)))
        return sums[-1]

    mine, theirs, parts = exchange(
        "join2", "fold2", after(head_x[0], keep), keep, send, keep, last_bits, "fjfj", 2, multiply
    )
    (total,) = sums
    far_cells = forward(after(pair_cells, total))
    (total,) = local("sum2", add_kernel, band_sum, (), (after(total, mine), pair, pair_cells))
    outs = band_sum + ([head_sum] if size else [])
    sums = (*parts, head_scale) if size else ()
    band_out, *head_out = local(
        "last",
        functools.partial(last_kernel, head_dev=size),
        outs,
        (),
        (total, far, far_cells, masked, mine, theirs, scale, *sums),
        [head_scratch],
    )
    if size:
        (head_out,) = head_out
    else:
        head_out = jnp.maximum(lax.psum_scatter(keep, "rows", scatter_dimension=0, tiled=True) * head_scale, 0.0)
    return band_out, head_out


def solution(mesh):
    in_specs = (
        P("rows", "feat"),
        P("rows", "feat"),
        P(None, None, "feat"),
        P("rows", None),
        P("rows", None, None),
        P("rows", None),
        P("rows"),
        P(None, "rows"),
        P("rows"),
        P(),
    )
    out_specs = (P("rows", "feat"), P("rows", "feat"))
    return jax.shard_map(body, mesh=mesh, in_specs=in_specs, out_specs=out_specs, check_vma=False)
```

```python
import functools

import jax
import jax.numpy as jnp
from jax import lax
from jax.experimental import pallas as pl
from jax.experimental.pallas import tpu as pltpu
from jax.sharding import PartitionSpec as P

BF = jnp.bfloat16
F32 = jnp.float32
LIMIT = 16 * 1024 * 1024
WORK = {
    "cast": 1_000_000,
    "part1": 2_000_000_000,
    "own": 10_000,
    "dense": 1_000_000,
    "join1": 200_000_000,
    "fold1": 2_000_000_000,
    "sum1": 1_000_000,
    "first": 1_000_000,
    "scale": 500_000_000,
    "begin": 1_000_000,
    "mid": 200_000_000,
    "end": 500_000_000,
    "part2": 1_000_000,
    "near": 500_000_000,
    "join2": 10_000,
    "fold2": 4_000_000_000,
    "sum2": 2_000_000_000,
    "last": 500_000_000,
    "collect": 500_000_000,
    "join3": 500_000_000,
    "headmix": 500_000_000,
}


def local(name, kernel, outs, scalars, args, scratch=()):
    vmem = pl.BlockSpec(memory_space=pltpu.VMEM)
    smem = pl.BlockSpec(memory_space=pltpu.SMEM)
    moved = sum(a.size * a.dtype.itemsize for a in args)
    return pl.pallas_call(
        kernel,
        out_shape=[jax.ShapeDtypeStruct(s, d) for s, d in outs],
        in_specs=[smem] * len(scalars) + [vmem] * len(args),
        out_specs=[vmem] * len(outs),
        scratch_shapes=list(scratch),
        cost_estimate=pl.CostEstimate(flops=WORK[name], bytes_accessed=moved, transcendentals=0),
        compiler_params=pltpu.CompilerParams(vmem_limit_bytes=LIMIT),
    )(*scalars, *args)


def mm(a, b):
    return jnp.dot(a, b, preferred_element_type=F32)


def swap(cells, axis, bit):
    count = lax.axis_size(axis)
    return lax.ppermute(cells, axis, [(i, i ^ bit) for i in range(count)])


def forward(cells):
    count = lax.axis_size("rows")
    pairs = []
    for i in range(count):
        if i % 2 == 0:
            pairs.append((i, i + 2 if i + 2 < count else i + 1))
        else:
            pairs.append((i, i - 2 if i > 1 else 0))
    return lax.ppermute(cells, "rows", pairs)


def spread(axis, cells, bits):
    pieces = {0: cells}
    for bit in bits:
        pieces.update({k | bit: swap(c, axis, bit) for k, c in list(pieces.items())})
    return pieces


def column(values, width):
    wide = jnp.broadcast_to(values.astype(F32), (128, values.shape[1]))
    tall = wide.T
    return jnp.concatenate([tall] * (width // 128), axis=1) if width > 128 else tall


def after(value, *others):
    return lax.optimization_barrier((value, *others))[0]


def xor_order(count):
    order = [0]
    bit = count // 2
    while bit:
        order += [k | bit for k in order]
        bit //= 2
    return order


def split_partial(part, keep, send, head_dev, bits):
    if not head_dev:
        keep[...] = part[...]
        send[...] = part[...].astype(BF)
        return
    half = len(bits) - 1
    for n in range(2 << half):
        owner = lax.axis_index("rows") ^ sum(bit for i, bit in enumerate(bits) if n >> (half - i) & 1)
        rows = part[pl.ds(pl.multiple_of(owner * head_dev, head_dev), head_dev)]
        if n < 1 << half:
            keep[n * head_dev : (n + 1) * head_dev] = rows
        else:
            n -= 1 << half
            send[n * head_dev : (n + 1) * head_dev] = rows.astype(BF)


def cast_kernel(cells, out):
    out[...] = cells[...].astype(BF)


def partial_kernel(rows, cells, *refs, head_dev, bits):
    keep, send, part = refs[-3:]
    if len(refs) > 3:
        refs[1][...] = refs[0][...].astype(BF)
    part[...] = mm(rows[...], cells[...])
    split_partial(part, keep, send, head_dev, bits)


def dense_kernel(place, tiles, near, pair, far, window, *, blocks):
    tile = tiles.shape[1]
    rows = window.shape[0]
    tile_rows = rows // tile
    parity = lax.axis_index("rows") % 2
    toward = 1 - 2 * parity
    inside = jnp.logical_and(lax.axis_index("rows") != 0, lax.axis_index("rows") != blocks - 1)
    window[...] = jnp.zeros_like(window)

    def add(s, carry):
        offset = place[2, s]
        group = jnp.where(offset == 0, 0, jnp.where(offset == toward, 1, 2))

        @pl.when(jnp.logical_or(group != 2, inside))
        def _():
            r = pl.ds(pl.multiple_of(place[0, s] * tile, tile), tile)
            c = pl.ds(pl.multiple_of((group * tile_rows + place[1, s]) * tile, tile), tile)
            window[r, c] += tiles[s].astype(F32)

        return carry

    lax.fori_loop(0, tiles.shape[0], add, 0)
    near[...] = window[:, :rows].astype(BF)
    pair[...] = window[:, rows : 2 * rows].astype(BF)
    far[...] = window[:, 2 * rows :].astype(BF)


def own_kernel(cols, reach, near, cells, masked, own):
    rows = masked.shape[0]
    limit = column(reach[...], 128)
    for g in range(cols.shape[1] // 128):
        here = slice(g * 128, (g + 1) * 128)
        lane = (lax.broadcasted_iota(jnp.int32, (rows, 128), 1) + g * 128).astype(F32)
        masked[:, here] = jnp.where(lane < limit, cols[:, here].astype(F32), 0.0).astype(BF)
    own[...] = mm(near[...], cells[...])


def near_kernel(near, cells, out):
    out[...] = mm(near[...], cells[...])


def sum_kernel(total, pair, cells, masked, mine, theirs, out, heads, *, head_dev):
    whole_heads(mine, theirs, heads, head_dev)
    out[...] = total[...] + mm(pair[...], cells[...]) + mm(masked[...], heads[...])


def fold_kernel(keep, arrived, kept, send):
    half = kept.shape[0]
    kept[...] = keep[:half] + arrived[:half].astype(F32)
    send[...] = (keep[half:] + arrived[half:].astype(F32)).astype(BF)


def join_kernel(*refs):
    size = refs[0].shape[0]
    for k, ref in enumerate(refs[:-1]):
        refs[-1][k * size : (k + 1) * size] = ref[...]


def whole_heads(mine, theirs, heads, head_dev):
    if not head_dev:
        heads[...] = mine[...]
        return
    pair, parity = lax.axis_index("rows") // 2, lax.axis_index("rows") % 2
    for n, k in enumerate(xor_order(mine.shape[0] // head_dev)):
        here = slice(n * head_dev, (n + 1) * head_dev)
        a = pl.multiple_of((2 * (pair ^ k) + parity) * head_dev, head_dev)
        b = pl.multiple_of((2 * (pair ^ k) + 1 - parity) * head_dev, head_dev)
        heads[pl.ds(a, head_dev)] = mine[here]
        heads[pl.ds(b, head_dev)] = theirs[here]


def first_sum_kernel(total, far, other, *refs):
    parts, out = refs[:-1], refs[-1]
    rows = total.shape[0]
    out[:rows] = (total[...] + mm(far[...], other[...])).astype(BF)
    if parts:
        extra = parts[0][...]
        for part in parts[1:]:
            extra = extra + part[...].astype(F32)
        out[rows:] = extra.astype(BF)


def add_kernel(total, pair, cells, out):
    out[...] = total[...] + mm(pair[...], cells[...])


def last_kernel(total, far, other, masked, mine, theirs, scale, *refs, head_dev):
    if head_dev:
        own, arrived, head_scale, out, head_out, heads = refs
        head_out[...] = jnp.maximum((own[...] + arrived[...].astype(F32)) * head_scale[...], 0.0)
    else:
        out, heads = refs
    whole_heads(mine, theirs, heads, head_dev)
    band = total[...] + mm(far[...], other[...]) + mm(masked[...], heads[...])
    out[...] = jnp.maximum(band * scale[...], 0.0)


def feature_rows(k, width):
    return pl.ds(pl.multiple_of((lax.axis_index("feat") ^ k) * width, width), width)


def mix_begin_kernel(*refs, early):
    half = (len(refs) - early) // 2
    pieces, shards, outs = refs[:early], refs[early : early + half], refs[early + half :]
    for shard, out in zip(shards, outs):
        total = None
        for k, piece in enumerate(pieces):
            term = mm(piece[...], shard[feature_rows(k, out.shape[1])])
            total = term if total is None else total + term
        out[...] = total


def mix_end_kernel(*refs, early, order, head_dev):
    pieces, refs = refs[:early], refs[early:]
    shards, refs = refs[: 2 * early], refs[2 * early :]
    begun, refs = refs[: 2 * early], refs[2 * early :]
    weights, band_scale, head_scale, *outs, scale = refs
    band, width = band_scale.shape
    scale[:band] = band_scale[...]
    if head_dev:
        scale[band:] = head_scale[...]
    result = None
    for n, (j, shard) in enumerate(zip(order, shards)):
        total = begun[n][...]
        for k, piece in enumerate(pieces):
            total = total + mm(piece[...], shard[feature_rows(early + k, width)])
        state = jnp.maximum(total * scale[...], 0.0).astype(BF)
        term = mm(state, weights[1, feature_rows(j, width)])
        result = term if result is None else result + term
    outs[0][...] = result[:band].astype(BF)
    if head_dev:
        outs[1][...] = result[band:].astype(BF)


def scale_kernel(degree, head_degree, scale, head_scale, all_scales):
    size = head_scale.shape[0]
    scale[...] = lax.rsqrt(column(degree[...], scale.shape[1]))
    all_scales[...] = lax.rsqrt(column(head_degree[...], scale.shape[1]))
    head_scale[...] = all_scales[pl.ds(pl.multiple_of(lax.axis_index("rows") * size, size), size)]


def wide_scale_kernel(degree, scale):
    scale[...] = lax.rsqrt(column(degree[...], scale.shape[1]))


def body(
    band_feats,
    head_feats,
    mix_weights,
    tile_place,
    tile_vals,
    arrow_cols,
    arrow_reach,
    arrow_rows,
    band_degree,
    head_degree,
):
    rows_dev, width = band_feats.shape
    head_dev = head_feats.shape[0]
    heads = arrow_cols.shape[1]
    blocks = lax.axis_size("rows")
    pairs = blocks // 2
    top_bit = lax.axis_size("feat") // 2
    low_bits = [1 << n for n in reversed(range(top_bit.bit_length() - 1))]
    reach = arrow_reach[None, :]
    size = head_dev if pairs <= 4 and head_dev % 16 == 0 else 0
    part_rows = heads // 2 if size else heads
    index_bits = [1 << n for n in range(blocks.bit_length() - 1)]
    bits, last_bits = [*index_bits[1:2], index_bits[0], *index_bits[2:]], [*index_bits[1:2], index_bits[0], *index_bits[2:]]
    part_scratch = pltpu.VMEM((heads, width), F32)
    head_scratch = pltpu.VMEM((heads, width), BF)
    band_sum = [((rows_dev, width), F32)]
    cells_shape = ((rows_dev, width), BF)
    head_sum = ((head_dev, width), F32)
    keep_shapes = [((part_rows, width), F32), ((part_rows, width), BF)]
    sum_up = functools.partial(sum_kernel, head_dev=size)

    def partial_sums(name, bits, cells, *head):
        outs = [(h.shape, BF) for h in head] + keep_shapes
        add_up = functools.partial(partial_kernel, head_dev=size, bits=bits)
        return local(name, add_up, outs, (), (arrow_rows, cells, *head), [part_scratch])

    def join(name, mine, other, before):
        shape = ((2 * mine.shape[0], width), BF)
        return local(name, join_kernel, [shape], (), (after(mine, before), other))[0]

    def fold(name, keep, arrived, before):
        rows = keep.shape[0] // 2
        outs = [((rows, width), F32), ((rows, width), BF)]
        return local(name, fold_kernel, outs, (), (after(keep, before), arrived))

    def exchange(joining, folding, own, keep, send, before, bits, turns, pause, between):
        if not size:
            between(before)
            everyone = lax.all_gather(own, "rows", axis=0, tiled=True)
            return everyone, everyone, []
        mine, gathers, halves = own, list(index_bits[:0:-1]), list(bits)
        other = swap(mine, "rows", gathers.pop(0))
        arrived = swap(send, "rows", halves.pop(0))
        for n, turn in enumerate(turns):
            if n == pause:
                before = between(before)
            if turn == "j":
                mine = before = join(joining, mine, other, before)
                other = swap(mine, "rows", gathers.pop(0) if gathers else 1)
            else:
                keep, send = fold(folding, keep, arrived, before)
                before = keep
                arrived = swap(send, "rows", halves.pop(0))
        if pause == len(turns):
            between(before)
        return mine, other, [keep, arrived]

    (cells,) = local("cast", cast_kernel, [cells_shape], (), (band_feats,))
    pair_cells = swap(cells, "rows", 1)
    first = after(mix_weights, cells)[0]
    across = swap(first, "feat", top_bit)
    head_cells, keep, send = partial_sums("part1", bits, cells, head_feats)
    first_part = keep
    laid = []

    def lay_out(before):
        outs = [((rows_dev, rows_dev), BF)] * 3
        args = (after(tile_vals, before),)
        scratch = [pltpu.VMEM((rows_dev, 3 * rows_dev), F32)]
        kernel = functools.partial(dense_kernel, blocks=blocks)
        laid.extend(local("dense", kernel, outs, (tile_place.T,), args, scratch))
        return laid[-1]

    mine, theirs, parts = exchange(
        "join1", "fold1", head_cells, keep, send, keep, bits, "jfjf", 2, lay_out
    )
    near, pair, far = laid
    masked, total = local(
        "own",
        own_kernel,
        [((rows_dev, heads), BF)] + band_sum,
        (),
        (arrow_cols, reach, after(near, *parts[:1]), cells),
    )
    far_cells = forward(after(pair_cells, first_part))
    (total,) = local(
        "sum1", sum_up, band_sum, (), (total, pair, pair_cells, masked, mine, theirs), [head_scratch]
    )
    tall = rows_dev + size
    (joined,) = local(
        "first", first_sum_kernel, [((tall, width), BF)], (), (total, far, far_cells, *parts)
    )

    opposite = swap(joined, "feat", top_bit)
    band_degree = after(band_degree, joined)
    if size:
        scale, head_scale = local(
            "scale",
            scale_kernel,
            band_sum + [head_sum],
            (),
            (band_degree[None, :], head_degree[None, :]),
            [pltpu.VMEM((heads, width), F32)],
        )
    else:
        (scale,) = local("scale", wide_scale_kernel, band_sum, (), (band_degree[None, :],))
        head_scale = lax.rsqrt(head_degree.astype(F32))[:, None] * jnp.ones((1, width), F32)
        head_scale = lax.dynamic_slice_in_dim(head_scale, lax.axis_index("rows") * head_dev, head_dev, 0)
    pieces = spread("feat", after(joined, scale), low_bits)
    early = len(pieces)
    pieces.update({k | top_bit: c for k, c in spread("feat", opposite, low_bits).items()})
    pieces = [pieces[k] for k in sorted(pieces)]
    shards = spread("feat", after(first, scale), low_bits)
    shards.update({k | top_bit: w for k, w in spread("feat", after(across, scale), low_bits).items()})
    order = [0, top_bit] + [k for k in sorted(shards) if k not in (0, top_bit)]
    begun = local(
        "begin",
        functools.partial(mix_begin_kernel, early=early),
        [((tall, width), F32)] * 2,
        (),
        (after(pieces[0], opposite), *pieces[1:early], shards[0], shards[top_bit]),
    )
    if len(order) > 2:
        begun += local(
            "mid",
            functools.partial(mix_begin_kernel, early=early),
            [((tall, width), F32)] * (len(order) - 2),
            (),
            (after(pieces[0], begun[0]), *pieces[1:early], *[shards[k] for k in order[2:]]),
        )
    cells, *head_x = local(
        "end",
        functools.partial(mix_end_kernel, early=early, order=order, head_dev=size),
        [cells_shape] + ([((size, width), BF)] if size else []),
        (),
        (*pieces[early:], *[shards[k] for k in order], *begun, mix_weights, scale, head_scale),
        [pltpu.VMEM((tall, width), F32)],
    )
    if not size:
        summed = lax.psum_scatter(first_part, "rows", scatter_dimension=0, tiled=True).astype(BF)
        summed = lax.all_gather(summed, "feat", axis=1, tiled=True)
        full = lax.all_gather(mix_weights[0], "feat", axis=1, tiled=True)
        head_state = jnp.maximum(mm(summed, full) * head_scale[:, :1], 0.0).astype(BF)
        head_x = [mm(head_state, mix_weights[1]).astype(BF)]

    keep, send = partial_sums("part2", last_bits, cells)
    pair_cells = swap(after(cells, keep), "rows", 1)
    sums = []

    def multiply(before):
        sums.extend(local("near", near_kernel, band_sum, (), (after(near, before), cells)))
        return sums[-1]

    mine, theirs, parts = exchange(
        "join2", "fold2", after(head_x[0], keep), keep, send, keep, last_bits, "fjfj", 2, multiply
    )
    (total,) = sums
    far_cells = forward(after(pair_cells, total))
    (total,) = local("sum2", add_kernel, band_sum, (), (after(total, mine), pair, pair_cells))
    outs = band_sum + ([head_sum] if size else [])
    sums = (*parts, head_scale) if size else ()
    band_out, *head_out = local(
        "last",
        functools.partial(last_kernel, head_dev=size),
        outs,
        (),
        (total, far, far_cells, masked, mine, theirs, scale, *sums),
        [head_scratch],
    )
    if size:
        (head_out,) = head_out
    else:
        head_out = jnp.maximum(lax.psum_scatter(keep, "rows", scatter_dimension=0, tiled=True) * head_scale, 0.0)
    return band_out, head_out


def solution(mesh):
    in_specs = (
        P("rows", "feat"),
        P("rows", "feat"),
        P(None, None, "feat"),
        P("rows", None),
        P("rows", None, None),
        P("rows", None),
        P("rows"),
        P(None, "rows"),
        P("rows"),
        P(),
    )
    out_specs = (P("rows", "feat"), P("rows", "feat"))
    return jax.shard_map(body, mesh=mesh, in_specs=in_specs, out_specs=out_specs, check_vma=False)
```
